128 devices in a mesh: dp: 8 (over x, core), group: 16 (over z, y).
Axes of the slice: x: 4, y: 4, z: 4, core: 2. Of those that a mesh axis runs over, the one named last changes fastest.
Arguments:
- gradients: bfloat16 [8, 16, 512, 512], P('dp', 'group'), may hold values from -1 to 1
- block_order: int32 [16], replicated, may hold values from 0 to 15, each once
- owner_count: int32 [16], replicated, may hold values from 0 to 3, as said below
- stat_left: float32 [16, 3, 512, 512], P('group', None, 'dp'), may hold values from -24 to 24
- stat_right: float32 [16, 3, 512, 512], P('group', None, 'dp'), may hold values from -24 to 24
- root_left: float32 [16, 3, 512, 512], P('group', None, 'dp')
- root_right: float32 [16, 3, 512, 512], P('group', None, 'dp')
- momentum: float32 [16, 3, 512, 512], P('group', None, 'dp'), may hold values from -3 to 3
Outputs:
- update_blocks: bfloat16 [16, 512, 512], replicated
- left_stats: float32 [16, 3, 512, 512], P('group', None, 'dp')
- right_stats: float32 [16, 3, 512, 512], P('group', None, 'dp')
- new_momentum: float32 [16, 3, 512, 512], P('group', None, 'dp')
The draws below stay inside these ranges and needn't reach their ends.
Inputs may be any that keep to these rules, and one draw needn't show every extreme that they name: `block_order`: each block index appears once. `owner_count`: the counts sum to 16; some owner holds exactly 3 blocks.
All inputs are finite; a program needn't handle non-finite values.
Results may differ from the reference program's by a relative error of at most 0.018.
Values may be sent and summed in bfloat16 or wider, within the bound.
No kernel may reach another device: no remote copies, remote signals or barrier semaphores. Data moves between devices by JAX's collectives and lax.ppermute only.
A program may use at most 64 MiB of HBM per device.

```python
import math
import jax
import jax.numpy as jnp
from jax import lax

BS = 512
MOST = 3
NB = 16
OWNERS = 16
REPLICAS = 8
N_GROUP = 16


def draw_owner_count(key, part):
    key = jax.random.fold_in(key, 5)
    first_key, second_key = jax.random.split(key)
    ticket_owner = jnp.arange(N_GROUP * MOST, dtype=jnp.int32) // MOST
    forced = jax.random.randint(first_key, (), 0, N_GROUP, dtype=jnp.int32)
    shuffled = jax.random.permutation(second_key, N_GROUP * MOST).astype(jnp.int32)
    priority = jnp.where(ticket_owner == forced, -1, shuffled)
    ordering = jnp.argsort(priority, stable=True)
    chosen = ticket_owner[ordering[:NB]]
    owners_range = jnp.arange(N_GROUP, dtype=jnp.int32)
    return jnp.sum((chosen[:, None] == owners_range[None, :]).astype(jnp.int32), axis=0, dtype=jnp.int32)


def scaled_root(key, noise_field, row_spread):
    sub_keys = jax.random.split(key, 3)
    diagonal = jax.random.uniform(sub_keys[0], (N_GROUP, MOST, BS), jnp.float32, 0.5, 2.0)
    rising = 3.0 ** (jnp.arange(BS, dtype=jnp.float32) / (BS - 1))
    row_scale = rising * jnp.exp(jax.random.uniform(sub_keys[1], (N_GROUP, MOST, BS), jnp.float32, 0.0, math.log(row_spread)))
    column_scale = jnp.exp(jax.random.uniform(sub_keys[2], (N_GROUP, MOST, BS), jnp.float32, 0.0, math.log(3.0)))
    identity = jnp.eye(BS, dtype=jnp.float32)
    matrix_core = identity * diagonal[..., None] + noise_field * (0.5 / math.sqrt(BS))
    return row_scale[..., None] * matrix_core * column_scale[..., None, :]


def draw_root_left(key, part):
    key = jax.random.fold_in(key, 11)
    noise_key, scale_key = jax.random.split(key)
    full_shape = (N_GROUP, MOST, BS, BS)
    noise_field = jax.random.normal(noise_key, full_shape, jnp.float32)
    return scaled_root(scale_key, noise_field, 3.3)


def draw_root_right(key, part):
    key = jax.random.fold_in(key, 23)
    noise_key, scale_key = jax.random.split(key)
    full_shape = (N_GROUP, MOST, BS, BS)
    noise_field = jax.random.normal(noise_key, full_shape, jnp.float32)
    return scaled_root(scale_key, noise_field, 3.3)


def strengthened(result, key, source, target, blocks, factor):
    def block_of(dim):
        return (jnp.arange(result.shape[dim]) // (result.shape[dim] // blocks)).reshape((-1,) + (1,) * (result.ndim - 1 - dim))

    first = jax.random.permutation(key, blocks)[block_of(target)]
    far = (block_of(target) + blocks // 2) % blocks
    return jnp.where((block_of(source) == first) | (block_of(source) == far), factor * result, result)


def steps_of(rng, extent, pieces, low, top_value):
    gain, own = 1.0, jax.random.fold_in(rng, 6)
    for dim, parts in pieces:
        heights = jnp.exp(jax.random.uniform(jax.random.fold_in(own, dim), (parts,), jnp.float32, low / len(pieces), top_value / len(pieces)))
        gain = gain * jnp.repeat(heights, extent[dim] // parts).reshape([-1 if axis == dim else 1 for axis in range(len(extent))])
    return gain


def centred(stream_key, extent, deviation, reach, shards=(), kind=jnp.bfloat16):
    drawn = deviation * jax.random.normal(stream_key, extent, jnp.float32)
    if shards:
        drawn = drawn * steps_of(stream_key, extent, shards, -0.22, 0.18)
    return jnp.clip(drawn, -reach, reach).astype(kind)


def heavy_noise(stream_key, extent, width, reach, shards, heavy, kind=jnp.bfloat16):
    drawn = width * jax.random.normal(stream_key, extent, jnp.float32)
    if shards:
        drawn = drawn * steps_of(stream_key, extent, shards, -0.22, 0.18)
    return jnp.clip(strengthened(drawn, jax.random.fold_in(stream_key, 3), *heavy), -reach, reach).astype(kind)


def setup_inputs(seed: int = 0) -> dict:
    key_of = jax.random.split(jax.random.key(seed), 9)
    return {
        "gradients": heavy_noise(key_of[0], (REPLICAS, NB, BS, BS), 0.18, 1.0, ((0, 8), (1, 16)), (0, 2, 8, 2.0)),
        "block_order": jax.random.permutation(key_of[1], NB).astype(jnp.int32),
        "owner_count": draw_owner_count(jax.random.fold_in(key_of[8], 71), 0),
        "stat_left": centred(key_of[3], (OWNERS, MOST, BS, BS), 4.0, 24.0, ((0, 16), (2, 8)), jnp.float32),
        "stat_right": centred(key_of[4], (OWNERS, MOST, BS, BS), 4.0, 24.0, ((0, 16), (2, 8)), jnp.float32),
        "root_left": draw_root_left(jax.random.fold_in(key_of[8], 71), 0),
        "root_right": draw_root_right(jax.random.fold_in(key_of[8], 71), 0),
        "momentum": centred(key_of[7], (OWNERS, MOST, BS, BS), 0.5, 3.0, ((0, 16), (2, 8)), jnp.float32),
    }


decay_stats = 0.95
decay_moment = 0.9
epsilon = 1e-06

def assignment(block_order, owner_count):
    range_ends = jnp.cumsum(owner_count, dtype=jnp.int32)
    range_starts = range_ends - owner_count
    slot_range = jnp.arange(MOST, dtype=jnp.int32)
    position = range_starts[:, None] + slot_range[None, :]
    slot_valid = slot_range[None, :] < owner_count[:, None]
    slot_blocks = block_order[jnp.minimum(position, NB - 1).astype(jnp.int32)]
    places = jnp.arange(NB, dtype=jnp.int32)
    block_place = lax.optimization_barrier(jnp.sum(jnp.where(block_order[None, :] == places[:, None], places[None, :], 0), axis=1, dtype=jnp.int32))
    block_owner = lax.optimization_barrier(jnp.sum((range_ends[None, :] <= block_place[:, None]).astype(jnp.int32), axis=1, dtype=jnp.int32))
    block_slot = block_owner * MOST + block_place - range_starts[block_owner]
    return (slot_blocks, slot_valid, block_slot)

def reference(gradients, block_order, owner_count, stat_left, stat_right, root_left, root_right, momentum):
    slot_blocks, slot_valid, block_slot = assignment(block_order, owner_count)
    live_mask = slot_valid[:, :, None, None]
    summed = lax.optimization_barrier(jnp.sum(gradients.astype(jnp.float32), axis=0)).astype(jnp.bfloat16)
    gradient = jnp.where(live_mask, summed[slot_blocks], jnp.zeros((), jnp.bfloat16))
    widened = lax.optimization_barrier(gradient).astype(jnp.float32)
    left_term = jnp.einsum('osik,osjk->osij', widened, widened)
    right_term = jnp.einsum('oski,oskj->osij', widened, widened)
    left_stats = jnp.where(live_mask, decay_stats * stat_left + (1.0 - decay_stats) * left_term, stat_left)
    right_stats = jnp.where(live_mask, decay_stats * stat_right + (1.0 - decay_stats) * right_term, stat_right)
    left_root = lax.optimization_barrier(root_left.astype(jnp.bfloat16)).astype(jnp.float32)
    right_root = lax.optimization_barrier(root_right.astype(jnp.bfloat16)).astype(jnp.float32)
    precond = jnp.einsum('osik,oskj->osij', left_root, widened).astype(jnp.bfloat16)
    precond = lax.optimization_barrier(precond).astype(jnp.float32)
    direction = jnp.einsum('osik,oskj->osij', precond, right_root)
    entries = float(BS * BS)
    grad_square = lax.optimization_barrier(jnp.sum(widened * widened, axis=(2, 3)))
    dir_square = lax.optimization_barrier(jnp.sum(direction * direction, axis=(2, 3)))
    graft = jnp.sqrt(grad_square / entries) / jnp.sqrt(dir_square / entries + epsilon)
    new_momentum = jnp.where(live_mask, decay_moment * momentum + graft[:, :, None, None] * direction, momentum)
    flat_slots = new_momentum.reshape(N_GROUP * MOST, BS, BS)
    update_blocks = flat_slots[block_slot].astype(jnp.bfloat16)
    return (update_blocks, left_stats, right_stats, new_momentum)
```

```python
import jax
import jax.numpy as jnp
from jax import lax
from jax.experimental import pallas as pl
from jax.experimental.pallas import tpu as pltpu
from jax.sharding import PartitionSpec as P

decay_stats = 0.95
decay_moment = 0.9
epsilon = 1e-06

AXES = ("dp", "group")
X, CORES, SIDE, SLOTS = 4, 2, 4, 3
BLOCKS = SIDE * SIDE
BS = 512
ROWS = BS // (X * CORES)
HALF = BS // CORES


def permute(value, target):
    pairs = []
    for x in range(X):
        for c in range(CORES):
            for z in range(SIDE):
                for y in range(SIDE):
                    tx, tc, tz, ty = target(x, c, z, y)
                    pairs.append(
                        ((x * 2 + c) * 16 + z * 4 + y, ((tx % 4) * 2 + tc) * 16 + (tz % 4) * 4 + ty % 4)
                    )
    return lax.ppermute(value, AXES, pairs)


def to_core(value):
    return permute(value, lambda x, c, z, y: (x, 1 - c, z, y))


def to_x(value, k):
    return permute(value, lambda x, c, z, y: (x + k, c, z, y))


def to_u(value, k):
    return permute(value, lambda x, c, z, y: (x, c, z, y + k) if c == 0 else (x, c, z + k, y))


def to_v(value, k):
    return permute(value, lambda x, c, z, y: (x, c, z + k, y) if c == 0 else (x, c, z, y + k))


def pick(options, index):
    out = options[0]
    for n in range(1, len(options)):
        out = jnp.where(index == n, options[n], out)
    return out


def look_up(table, index):
    slots = jnp.arange(table.shape[0], dtype=jnp.int32)
    hit = slots == index[..., None]
    return jnp.sum(jnp.where(hit, table, 0), axis=-1, dtype=jnp.int32)


def fill_grad(c_ref, g_own, g_other, grad):
    c = c_ref[0]
    grad[pl.ds(pl.multiple_of(c * HALF, HALF), HALF), :] = g_own[...]
    grad[pl.ds(pl.multiple_of((1 - c) * HALF, HALF), HALF), :] = g_other[...]


def step_kernel(c_ref, g_own, g_other, a_own, a_other, out, grad, full):
    c = c_ref[0]
    fill_grad(c_ref, g_own, g_other, grad)
    for n in range(3):
        for x in range(X):
            full[n, pl.ds(pl.multiple_of((2 * x + c) * ROWS, ROWS), ROWS), :] = a_own[n, x]
            full[n, pl.ds(pl.multiple_of((2 * x + 1 - c) * ROWS, ROWS), ROWS), :] = a_other[n, x]
    g = grad[...]
    wide = g.astype(jnp.float32)
    grad_square = jnp.sum(wide * wide)
    precond = jnp.dot(full[0], g, preferred_element_type=jnp.float32).astype(jnp.bfloat16)
    direction = jnp.dot(precond, full[1], preferred_element_type=jnp.float32)
    dir_square = jnp.sum(direction * direction)
    entries = float(BS * BS)
    top = jnp.sqrt(jnp.full((1, BS), grad_square / entries, jnp.float32))
    graft = top / jnp.sqrt(jnp.full((1, BS), dir_square / entries + epsilon, jnp.float32))
    out[...] = (decay_moment * full[2].astype(jnp.float32) + graft * direction).astype(jnp.bfloat16)


def term_kernel(c_ref, g_own, g_other, out, grad, held):
    fill_grad(c_ref, g_own, g_other, grad)
    c, x = c_ref[0], c_ref[1]
    g = grad[...]
    rows = grad[pl.ds(pl.multiple_of((2 * x + c) * ROWS, ROWS), ROWS), :]
    out[0] = lax.dot_general(
        rows, g, (((1,), (1,)), ((), ())), preferred_element_type=jnp.float32
    ).astype(jnp.bfloat16)
    columns = grad[:, pl.ds(pl.multiple_of(x * 2 * ROWS, 2 * ROWS), 2 * ROWS)]
    held[...] = lax.dot_general(
        columns, g, (((0,), (0,)), ((), ())), preferred_element_type=jnp.float32
    )
    out[1] = held[pl.ds(pl.multiple_of(c * ROWS, ROWS), ROWS), :].astype(jnp.bfloat16)


def place_kernel(where_ref, *refs):
    sources, out, sems = refs[:8], refs[8], refs[9]
    copies = []
    for n in range(8):
        for j in range(4):
            block = where_ref[n * 4 + j]
            half = where_ref[32] if n < 4 else 1 - where_ref[32]
            copies.append(
                pltpu.make_async_copy(
                    sources[n].at[j],
                    out.at[block, pl.ds(pl.multiple_of(half * HALF, HALF), HALF), :],
                    sems.at[n * 4 + j],
                )
            )
    for copy in copies:
        copy.start()
    for copy in copies:
        copy.wait()


SMEM = pl.BlockSpec(memory_space=pltpu.SMEM)
VMEM = pl.BlockSpec(memory_space=pltpu.VMEM)
ANY = pl.BlockSpec(memory_space=pl.ANY)


def local(
    gradients, block_order, owner_count, stat_left, stat_right, root_left, root_right, momentum
):
    dp = lax.axis_index("dp")
    me = lax.axis_index("group")
    x, c = dp // 2, dp % 2
    y, z = me % 4, me // 4
    first = c == 0
    u, v = jnp.where(first, y, z), jnp.where(first, z, y)

    def place_at(uu, vv):
        yy, zz = jnp.where(first, uu, vv), jnp.where(first, vv, uu)
        return 4 * ((zz - yy) % 4) + yy

    def uv_of_member(g):
        yy, zz = g % 4, g // 4
        return jnp.where(first, yy, zz), jnp.where(first, zz, yy)

    def uv_of_place(q):
        yy, zz = q % 4, (q % 4 + q // 4) % 4
        return jnp.where(first, yy, zz), jnp.where(first, zz, yy)

    four = jnp.arange(4, dtype=jnp.int32)
    three = jnp.arange(SLOTS, dtype=jnp.int32)
    ends = jnp.cumsum(owner_count, dtype=jnp.int32)
    starts = ends - owner_count
    places = jnp.arange(BLOCKS, dtype=jnp.int32)
    place_owner = jnp.sum((ends[None, :] <= places[:, None]).astype(jnp.int32), axis=1, dtype=jnp.int32)

    v_places = place_at(u, (v + four) % 4)
    v_blocks = look_up(block_order, v_places)
    v_owners = look_up(place_owner, v_places)
    block_u, block_v = uv_of_member(v_blocks)
    grad_pick = (u - block_u) % 4
    grad_last = (v - block_v[0]) % 4
    owner_u, owner_v = uv_of_member(v_owners)
    root_pick = (u - owner_u) % 4
    root_last = (v - owner_v[0]) % 4

    my_start, my_count = look_up(starts, me[None])[0], look_up(owner_count, me[None])[0]
    live = three < my_count
    slot_place = jnp.minimum(my_start + three, BLOCKS - 1)
    slot_block = look_up(block_order, slot_place)
    slot_u, _ = uv_of_place(slot_place)
    slot_pick = jnp.sum(
        jnp.where((slot_u[None, :] == ((u + four) % 4)[:, None]) & live[None, :], three[None, :], 0),
        axis=1,
    )
    term_last = (u - slot_u) % 4
    u_far = (u + four) % 4
    u_members = jnp.where(first, 4 * v + u_far, 4 * u_far + v)
    far_place = look_up(starts, u_members)[:, None] + three[None, :]
    far_live = three[None, :] < look_up(owner_count, u_members)[:, None]
    far_u, far_v = uv_of_place(far_place)
    term_pick = jnp.sum(jnp.where(far_live & (far_u == u), (v - far_v) % 4, 0), axis=1)

    own_places = place_at((u - four[None, :]) % 4, (v - four[:, None]) % 4)
    other_places = place_at((u - four[:, None]) % 4, (v - four[None, :]) % 4)
    landing = look_up(block_order, jnp.concatenate([own_places, other_places]).reshape(-1))
    landing = jnp.concatenate([landing, c[None]])
    spot = jnp.stack([c, x])

    halves = gradients[0, 0].reshape(2, HALF, BS)
    mine = lax.dynamic_index_in_dim(halves, c, 0, keepdims=False)
    theirs = lax.dynamic_index_in_dim(halves, 1 - c, 0, keepdims=False)
    pair = mine.astype(jnp.float32) + to_core(theirs).astype(jnp.float32)
    pair = pair.astype(jnp.bfloat16).reshape(X, ROWS, BS)
    total = lax.dynamic_index_in_dim(pair, x, 0, keepdims=False).astype(jnp.float32)
    for k in (1, 3, 2):
        part = lax.dynamic_index_in_dim(pair, (x + k) % 4, 0, keepdims=False)
        total = total + to_x(part, k).astype(jnp.float32)
    chunk = total.astype(jnp.bfloat16)

    def along(send, values):
        got = [values[0], None, None, None]
        for k in (2, 1, 3):
            got[k] = send(values[k], k)
        return got

    row = along(to_u, [chunk] * 4)
    column = along(to_v, [pick(row, grad_pick[k]) for k in range(4)])
    chunk = pick(column, grad_last)

    slots = jnp.stack([root_left[0], root_right[0], momentum[0]], axis=1).astype(jnp.bfloat16)
    packs = [lax.dynamic_index_in_dim(slots, slot_pick[k], 0, keepdims=False) for k in range(4)]
    row = along(to_u, packs)
    column = along(to_v, [pick(row, root_pick[k]) for k in range(4)])
    pack = pick(column, root_last)

    def over_x(value):
        got = along(to_x, [value] * 4)
        return jnp.stack([pick(got, (x - n) % 4) for n in range(4)], axis=-3)

    pack = over_x(pack)
    pack_other = to_core(pack)
    grad_own = over_x(chunk).reshape(HALF, BS)
    grad_other = to_core(grad_own)

    update = pl.pallas_call(
        step_kernel,
        out_shape=jax.ShapeDtypeStruct((BS, BS), jnp.bfloat16),
        in_specs=[SMEM, VMEM, VMEM, VMEM, VMEM],
        out_specs=VMEM,
        scratch_shapes=[
            pltpu.VMEM((BS, BS), jnp.bfloat16),
            pltpu.VMEM((3, BS, BS), jnp.bfloat16),
        ],
        compiler_params=pltpu.CompilerParams(vmem_limit_bytes=32 << 20),
        cost_estimate=pl.CostEstimate(flops=4 * BS**3, bytes_accessed=5 * BS * BS * 2, transcendentals=0),
        name="step",
    )(spot, grad_own, grad_other, pack, pack_other)

    terms = pl.pallas_call(
        term_kernel,
        out_shape=jax.ShapeDtypeStruct((2, ROWS, BS), jnp.bfloat16),
        in_specs=[SMEM, VMEM, VMEM],
        out_specs=VMEM,
        scratch_shapes=[
            pltpu.VMEM((BS, BS), jnp.bfloat16),
            pltpu.VMEM((2 * ROWS, BS), jnp.float32),
        ],
        compiler_params=pltpu.CompilerParams(vmem_limit_bytes=32 << 20),
        cost_estimate=pl.CostEstimate(
            flops=6 * ROWS * BS * BS, bytes_accessed=BS * BS * 2, transcendentals=0
        ),
        name="terms",
    )(spot, grad_own, grad_other)

    half = lax.dynamic_slice_in_dim(update, c * HALF, HALF, 0)
    near = jnp.stack(along(to_u, [half] * 4))
    held = along(to_v, [near] * 4)
    across = [to_core(value) for value in held]
    update_blocks = pl.pallas_call(
        place_kernel,
        out_shape=jax.ShapeDtypeStruct((BLOCKS, BS, BS), jnp.bfloat16),
        in_specs=[SMEM] + [ANY] * 8,
        out_specs=ANY,
        scratch_shapes=[pltpu.SemaphoreType.DMA((32,))],
        name="place",
    )(landing, *held, *across)

    column = along(to_v, [terms] * 4)
    row = along(to_u, [pick(column, term_pick[k]) for k in range(4)])
    back = jnp.stack([pick(row, term_last[s]) for s in range(SLOTS)]).astype(jnp.float32)

    alive = live[:, None, None]
    left_stats = jnp.where(
        alive, decay_stats * stat_left[0] + (1.0 - decay_stats) * back[:, 0], stat_left[0]
    )
    right_stats = jnp.where(
        alive, decay_stats * stat_right[0] + (1.0 - decay_stats) * back[:, 1], stat_right[0]
    )
    fresh = jnp.stack(
        [
            lax.dynamic_slice(update_blocks, (slot_block[s], dp * ROWS, 0), (1, ROWS, BS))[0]
            for s in range(SLOTS)
        ]
    )
    new_momentum = jnp.where(alive, fresh.astype(jnp.float32), momentum[0])
    return (update_blocks, left_stats[None], right_stats[None], new_momentum[None])


def solution(mesh):
    placed = (
        P("dp", "group", None, None),
        P(),
        P(),
        P("group", None, "dp", None),
        P("group", None, "dp", None),
        P("group", None, "dp", None),
        P("group", None, "dp", None),
        P("group", None, "dp", None),
    )
    return jax.shard_map(
        local,
        mesh=mesh,
        in_specs=placed,
        out_specs=(
            P(),
            P("group", None, "dp", None),
            P("group", None, "dp", None),
            P("group", None, "dp", None),
        ),
        check_vma=False,
    )
```

```python
import functools

import jax
import jax.numpy as jnp
from jax import lax
from jax.experimental import pallas as pl
from jax.experimental.pallas import tpu as pltpu
from jax.sharding import PartitionSpec as P

decay_stats = 0.95
decay_moment = 0.9
epsilon = 1e-06

AXES = ("dp", "group")
X, CORES, SIDE, SLOTS = 4, 2, 4, 3
BLOCKS = SIDE * SIDE
BS = 512
ROWS = BS // (X * CORES)
HALF = BS // CORES
NEAR = SIDE * HALF
half_type = jnp.bfloat16
wide_type = jnp.float32

SMEM = pl.BlockSpec(memory_space=pltpu.SMEM)
VMEM = pl.BlockSpec(memory_space=pltpu.VMEM)
ANY = pl.BlockSpec(memory_space=pl.ANY)

GRAD_PICK, GRAD_LAST, ROOT_PICK, ROOT_LAST = 0, 4, 5, 9
SLOT_PICK, TERM_PICK, TERM_LAST, SLOT_LIVE, SLOT_BLOCK, LANDING = 10, 14, 18, 21, 24, 27
CHOICES = LANDING + 32


def permute(value, target):
    pairs = []
    for x in range(X):
        for c in range(CORES):
            for z in range(SIDE):
                for y in range(SIDE):
                    tx, tc, tz, ty = target(x, c, z, y)
                    pairs.append(
                        ((x * 2 + c) * 16 + z * 4 + y, ((tx % 4) * 2 + tc) * 16 + (tz % 4) * 4 + ty % 4)
                    )
    return lax.ppermute(value, AXES, pairs)


def to_core(value):
    return permute(value, lambda x, c, z, y: (x, 1 - c, z, y))


def to_x(value, k):
    return permute(value, lambda x, c, z, y: (x + k, c, z, y))


def to_u(value, k):
    return permute(value, lambda x, c, z, y: (x, c, z, y + k) if c == 0 else (x, c, z + k, y))


def to_v(value, k):
    return permute(value, lambda x, c, z, y: (x, c, z + k, y) if c == 0 else (x, c, z, y + k))


def along(send, values):
    got = [values[0], None, None, None]
    for k in (1, 3, 2):
        got[k] = send(values[k], k)
    return got


def position():
    dp, me = lax.axis_index("dp"), lax.axis_index("group")
    return dp >> 1, dp & 1, me >> 2, me & 3


def choice_kernel(order_ref, count_ref, out, start_ref, owner_ref):
    x, c, z, y = position()
    me = z * 4 + y
    first = c == 0
    u, v = jnp.where(first, y, z), jnp.where(first, z, y)

    def place_at(uu, vv):
        yy, zz = jnp.where(first, uu, vv), jnp.where(first, vv, uu)
        return 4 * ((zz - yy) & 3) + yy

    def uv_of_member(g):
        yy, zz = g & 3, g >> 2
        return jnp.where(first, yy, zz), jnp.where(first, zz, yy)

    def uv_of_place(q):
        yy = q & 3
        zz = (yy + (q >> 2)) & 3
        return jnp.where(first, yy, zz), jnp.where(first, zz, yy)

    place = jnp.int32(0)
    for o in range(BLOCKS):
        start_ref[o] = place
        for s in range(SLOTS):

            @pl.when(s < count_ref[o])
            def _():
                owner_ref[start_ref[o] + s] = o

        place = place + count_ref[o]

    for k in range(4):
        q = place_at(u, (v + k) & 3)
        block = order_ref[q]
        bu, bv = uv_of_member(block)
        out[GRAD_PICK + k] = (u - bu) & 3
        ou, ov = uv_of_member(owner_ref[q])
        out[ROOT_PICK + k] = (u - ou) & 3
        if k == 0:
            out[GRAD_LAST] = (v - bv) & 3
            out[ROOT_LAST] = (v - ov) & 3
    my_start, my_count = start_ref[me], count_ref[me]
    slot_u = []
    for s in range(SLOTS):
        q = jnp.minimum(my_start + s, BLOCKS - 1)
        su, sv = uv_of_place(q)
        slot_u.append(su)
        out[TERM_LAST + s] = (v - sv) & 3
        out[SLOT_LIVE + s] = (s < my_count).astype(jnp.int32)
        out[SLOT_BLOCK + s] = order_ref[q]
    for k in range(4):
        far = (u + k) & 3
        chosen = jnp.int32(0)
        for s in range(SLOTS):
            chosen = jnp.where((s < my_count) & (slot_u[s] == far), s, chosen)
        out[SLOT_PICK + k] = chosen
        far = (v + k) & 3
        member = jnp.where(first, 4 * far + u, 4 * u + far)
        chosen = jnp.int32(0)
        for s in range(SLOTS):
            fu, fv = uv_of_place(start_ref[member] + s)
            chosen = jnp.where((s < count_ref[member]) & (fv == v), (u - fu) & 3, chosen)
        out[TERM_PICK + k] = chosen
    for k in range(4):
        for j in range(4):
            out[LANDING + k * 4 + j] = order_ref[place_at((u - j) & 3, (v - k) & 3)]
            out[LANDING + 16 + k * 4 + j] = order_ref[place_at((u - k) & 3, (v - j) & 3)]


def choices(block_order, owner_count):
    return pl.pallas_call(
        choice_kernel,
        out_shape=jax.ShapeDtypeStruct((CHOICES,), jnp.int32),
        in_specs=[SMEM, SMEM],
        out_specs=SMEM,
        scratch_shapes=[pltpu.SMEM((BLOCKS,), jnp.int32), pltpu.SMEM((BLOCKS,), jnp.int32)],
        name="choices",
    )(block_order, owner_count)


def cost(flops, *arrays):
    moved = sum(a.size * a.dtype.itemsize for a in arrays)
    return pl.CostEstimate(flops=flops, bytes_accessed=moved, transcendentals=0)


def small_call(body, outs, name, *args, aliases=None, flops=0, scratch=()):
    return pl.pallas_call(
        body,
        out_shape=outs,
        in_specs=[SMEM if a.dtype == jnp.int32 else VMEM for a in args],
        out_specs=jax.tree.map(lambda _: VMEM, outs),
        scratch_shapes=scratch,
        input_output_aliases=aliases or {},
        compiler_params=pltpu.CompilerParams(vmem_limit_bytes=12 << 20),
        cost_estimate=cost(flops, *args, *jax.tree.leaves(outs)),
        name=name,
    )(*args)


def copy_chosen(index, options, out, at):
    for n, option in enumerate(options):

        @pl.when(index == n)
        def _():
            out[...] = option[at]


def pair_kernel(mine, theirs, own, *sends):
    x, c, _, _ = position()
    for k in range(4):
        at = pl.ds(pl.multiple_of(c * HALF + ((x + k) & 3) * ROWS, ROWS), ROWS)
        both = mine[at, :].astype(wide_type) + theirs[at, :].astype(wide_type)
        if k == 0:
            own[...] = both
        else:
            sends[k - 1][...] = both.astype(half_type)


def pack_kernel(spot, left, right, moment, *outs):
    for k, out in enumerate(outs):
        slot = spot[SLOT_PICK + k]
        out[0] = left[slot].astype(half_type)
        out[1] = right[slot].astype(half_type)
        out[2] = moment[slot].astype(half_type)


def total_kernel(own, a, b, c, *packs):
    total = own[...] + a[...].astype(wide_type)
    total = total + b[...].astype(wide_type)
    total = (total + c[...].astype(wide_type)).astype(half_type)
    for out in packs[4:]:
        out[3] = total


def turn_kernel(spot, a, b, c, d, *outs):
    for k, out in enumerate(outs):
        copy_chosen(spot[ROOT_PICK + k], (a, b, c, d), out.at[:3], pl.ds(0, 3))
        copy_chosen(spot[GRAD_PICK + k], (a, b, c, d), out.at[3:], pl.ds(3, 1))


def here_kernel(spot, a, b, c, d, out):
    copy_chosen(spot[ROOT_LAST], (a, b, c, d), out.at[:3], pl.ds(0, 3))
    copy_chosen(spot[GRAD_LAST], (a, b, c, d), out.at[3:], pl.ds(3, 1))


def line_kernel(*refs):
    out = refs[4]
    x = position()[0]
    for k in range(4):
        out[(x - k) & 3] = refs[k][...]


def line_up(got, name):
    shape = jax.ShapeDtypeStruct((4,) + got[0].shape, got[0].dtype)
    return small_call(line_kernel, shape, name, *got)


def step_kernel(mine, other, out, grad, full, held):
    x, c, _, _ = position()
    for n in range(X):
        for core, source in ((c, mine), (1 - c, other)):
            rows = pl.ds(pl.multiple_of((2 * n + core) * ROWS, ROWS), ROWS)
            for which in range(3):
                full[which, rows, :] = source[n, which]
            grad[pl.ds(pl.multiple_of(core * HALF + n * ROWS, ROWS), ROWS), :] = source[n, 3]
    g = grad[...]
    wide = g.astype(wide_type)
    grad_square = jnp.sum(wide * wide)
    precond = jnp.dot(full[0], g, preferred_element_type=wide_type).astype(half_type)
    held[...] = jnp.dot(precond, full[1], preferred_element_type=wide_type)
    dir_square = jnp.sum(held[...] * held[...])
    entries = float(BS * BS)
    top = jnp.sqrt(jnp.full((1, BS), grad_square / entries, wide_type))
    graft = top / jnp.sqrt(jnp.full((1, BS), dir_square / entries + epsilon, wide_type))
    half = pl.ds(pl.multiple_of(c * HALF, HALF), HALF)
    fresh = decay_moment * full[2, half, :].astype(wide_type) + graft * held[half, :]
    out[:HALF, :] = fresh.astype(half_type)
    rows = grad[pl.ds(pl.multiple_of((2 * x + c) * ROWS, ROWS), ROWS), :]
    out[HALF : HALF + ROWS, :] = lax.dot_general(
        rows, g, (((1,), (1,)), ((), ())), preferred_element_type=wide_type
    ).astype(half_type)
    columns = grad[:, pl.ds(pl.multiple_of(x * 2 * ROWS, 2 * ROWS), 2 * ROWS)]
    held[: 2 * ROWS, :] = lax.dot_general(
        columns, g, (((0,), (0,)), ((), ())), preferred_element_type=wide_type
    )
    term = held[pl.ds(pl.multiple_of(c * ROWS, ROWS), ROWS), :]
    out[HALF + ROWS :, :] = term.astype(half_type)


def near_kernel(spot, a, b, c, d, *outs):
    for k, out in enumerate(outs):
        for j, source in enumerate((a, b, c, d)):
            out[j * HALF : (j + 1) * HALF, :] = source[:HALF, :]
        copy_chosen(spot[TERM_PICK + k], (a, b, c, d), out.at[NEAR:], pl.ds(HALF, 2 * ROWS))


def placed_copies(spot, sources, out, sems):
    _, c, _, _ = position()
    copies = []
    for n, (which, source) in enumerate(sources):
        half = c if which < 4 else 1 - c
        for j in range(4):
            copies.append(
                pltpu.make_async_copy(
                    source.at[pl.ds(j * HALF, HALF), :],
                    out.at[
                        spot[LANDING + which * 4 + j],
                        pl.ds(pl.multiple_of(half * HALF, HALF), HALF),
                        :,
                    ],
                    sems.at[n * 4 + j],
                )
            )
    return copies


def place_kernel(which, spot, *refs):
    mine, other, out, sems = refs[-4:]
    copies = placed_copies(spot, ((which, mine), (which + 4, other)), out, sems)
    for copy in copies:
        copy.start()
    for copy in copies:
        copy.wait()


def place(which, spot, begun, mine, other):
    given = [mine, other] if begun is None else [begun, mine, other]
    out = jax.ShapeDtypeStruct((BLOCKS, BS, BS), half_type)
    return pl.pallas_call(
        functools.partial(place_kernel, which),
        out_shape=out,
        in_specs=[SMEM] + [ANY] * (len(given) - 2) + [VMEM] * 2,
        out_specs=ANY,
        scratch_shapes=[pltpu.SemaphoreType.DMA((8,))],
        input_output_aliases={} if begun is None else {1: 0},
        compiler_params=pltpu.CompilerParams(vmem_limit_bytes=4 << 20),
        cost_estimate=cost(0, mine, other, mine, other),
        name="place",
    )(spot, *given)


def finish_kernel(spot, begun, moment, *refs):
    del begun
    sources, (out, out_moment, sems) = refs[:8], refs[8:]
    copies = placed_copies(
        spot, [(n, sources[n]) for n in (3, 2, 7, 6)], out, sems
    )
    for copy in copies:
        copy.start()
    x, c, _, _ = position()
    row = (2 * x + c) * ROWS
    in_half = row & (HALF - 1)
    for s in range(SLOTS):
        live = spot[SLOT_LIVE + s] == 1
        block = spot[SLOT_BLOCK + s]
        out_moment[s] = moment[s]
        for n, source in enumerate(sources):
            half = c if n < 4 else 1 - c
            for j in range(4):

                @pl.when(live & (spot[LANDING + n * 4 + j] == block) & ((row >> 8) == half))
                def _():
                    at = pl.ds(pl.multiple_of(j * HALF + in_half, ROWS), ROWS)
                    out_moment[s] = source[at, :].astype(wide_type)

    for copy in copies:
        copy.wait()


def stats_kernel(spot, left, right, *refs):
    sources, outs = refs[:4], refs[4:]
    for s in range(SLOTS):
        for old, out in zip((left, right), outs):
            out[s] = old[s]
        for n, source in enumerate(sources):

            @pl.when((spot[SLOT_LIVE + s] == 1) & (spot[TERM_LAST + s] == n))
            def _():
                for i, (old, out) in enumerate(zip((left, right), outs)):
                    at = pl.ds(NEAR + i * ROWS, ROWS)
                    term = source[at, :].astype(wide_type)
                    out[s] = decay_stats * old[s] + (1.0 - decay_stats) * term


def local(
    gradients, block_order, owner_count, stat_left, stat_right, root_left, root_right, momentum
):
    chunk_type = jax.ShapeDtypeStruct((ROWS, BS), half_type)
    pack_type = jax.ShapeDtypeStruct((4, ROWS, BS), half_type)
    stat_type = jax.ShapeDtypeStruct((SLOTS, ROWS, BS), wide_type)
    spot = choices(block_order, owner_count)
    hold = lax.optimization_barrier

    mine = gradients[0, 0]
    own, *sends = small_call(
        pair_kernel,
        [jax.ShapeDtypeStruct((ROWS, BS), wide_type)] + [chunk_type] * 3,
        "pair",
        mine,
        to_core(mine),
    )
    sends, left, right, moment = hold((sends, root_left[0], root_right[0], momentum[0]))
    packs = small_call(pack_kernel, [pack_type] * 4, "packs", spot, left, right, moment)
    got = along(to_x, [own] + sends)

    packs = small_call(
        total_kernel, [pack_type] * 4, "total", *got, *packs, aliases={4: 0, 5: 1, 6: 2, 7: 3}
    )
    row = along(to_u, packs)
    column = along(to_v, small_call(turn_kernel, [pack_type] * 4, "turn", spot, *row))
    pack = small_call(here_kernel, pack_type, "here", spot, *column)
    full = line_up(along(to_x, [pack] * 4), "line")
    send = small_call(
        step_kernel,
        jax.ShapeDtypeStruct((HALF + 2 * ROWS, BS), half_type),
        "step",
        full,
        to_core(full),
        flops=6 * BS**3,
        scratch=[
            pltpu.VMEM((BS, BS), half_type),
            pltpu.VMEM((3, BS, BS), half_type),
            pltpu.VMEM((BS, BS), wide_type),
        ],
    )

    row = along(to_u, [send] * 4)
    near_type = jax.ShapeDtypeStruct((NEAR + 2 * ROWS, BS), half_type)
    nears = small_call(near_kernel, [near_type] * 4, "near", spot, *row)
    held = along(to_v, nears)
    across = [to_core(value) for value in held]
    begun = place(0, spot, None, held[0], across[0])
    begun = place(1, spot, begun, held[1], across[1])
    left_stats, right_stats = small_call(
        stats_kernel, [stat_type] * 2, "stats", spot, stat_left[0], stat_right[0], *held
    )
    update_blocks, new_momentum = pl.pallas_call(
        finish_kernel,
        out_shape=[jax.ShapeDtypeStruct((BLOCKS, BS, BS), half_type), stat_type],
        in_specs=[SMEM, ANY] + [VMEM] * 9,
        out_specs=[ANY, VMEM],
        scratch_shapes=[pltpu.SemaphoreType.DMA((16,))],
        input_output_aliases={1: 0},
        compiler_params=pltpu.CompilerParams(vmem_limit_bytes=16 << 20),
        cost_estimate=cost(0, *held, *held),
        name="finish",
    )(spot, begun, momentum[0], *held, *across)
    return (update_blocks, left_stats[None], right_stats[None], new_momentum[None])


def solution(mesh):
    placed = (
        P("dp", "group", None, None),
        P(),
        P(),
        P("group", None, "dp", None),
        P("group", None, "dp", None),
        P("group", None, "dp", None),
        P("group", None, "dp", None),
        P("group", None, "dp", None),
    )
    return jax.shard_map(
        local,
        mesh=mesh,
        in_specs=placed,
        out_specs=(
            P(),
            P("group", None, "dp", None),
            P("group", None, "dp", None),
            P("group", None, "dp", None),
        ),
        check_vma=False,
    )
```

```python
import functools

import jax
import jax.numpy as jnp
from jax import lax
from jax.experimental import pallas as pl
from jax.experimental.pallas import tpu as pltpu
from jax.sharding import PartitionSpec as P

decay_stats = 0.95
decay_moment = 0.9
epsilon = 1e-06

AXES = ("dp", "group")
X, CORES, SIDE, SLOTS = 4, 2, 4, 3
BLOCKS = SIDE * SIDE
BS = 512
ROWS = BS // (X * CORES)
HALF = BS // CORES
NEAR = SIDE * HALF
half_type = jnp.bfloat16
wide_type = jnp.float32

SMEM = pl.BlockSpec(memory_space=pltpu.SMEM)
VMEM = pl.BlockSpec(memory_space=pltpu.VMEM)
ANY = pl.BlockSpec(memory_space=pl.ANY)

GRAD_PICK, GRAD_LAST, ROOT_PICK, ROOT_LAST = 0, 4, 5, 9
SLOT_PICK, TERM_PICK, TERM_LAST, SLOT_LIVE, SLOT_FROM, SLOT_ROW = 10, 14, 18, 21, 24, 27
LANDING = 30
CHOICES = LANDING + 32


def permute(value, target):
    pairs = []
    for x in range(X):
        for c in range(CORES):
            for z in range(SIDE):
                for y in range(SIDE):
                    tx, tc, tz, ty = target(x, c, z, y)
                    pairs.append(
                        ((x * 2 + c) * 16 + z * 4 + y, ((tx % 4) * 2 + tc) * 16 + (tz % 4) * 4 + ty % 4)
                    )
    return lax.ppermute(value, AXES, pairs)


def to_core(value):
    return permute(value, lambda x, c, z, y: (x, 1 - c, z, y))


def to_x(value, k):
    return permute(value, lambda x, c, z, y: (x + k, c, z, y))


def to_u(value, k):
    return permute(value, lambda x, c, z, y: (x, c, z, y + k) if c == 0 else (x, c, z + k, y))


def to_v(value, k):
    return permute(value, lambda x, c, z, y: (x, c, z + k, y) if c == 0 else (x, c, z, y + k))


def along(send, values, shifts=(1, 3, 2)):
    return [values[0]] + [send(values[k], k) for k in shifts]


def position():
    dp, me = lax.axis_index("dp"), lax.axis_index("group")
    return dp >> 1, dp & 1, me >> 2, me & 3


def choice_kernel(order_ref, count_ref, out, start_ref, owner_ref):
    x, c, z, y = position()
    me = z * 4 + y
    first = c == 0
    u, v = jnp.where(first, y, z), jnp.where(first, z, y)

    def place_at(uu, vv):
        yy, zz = jnp.where(first, uu, vv), jnp.where(first, vv, uu)
        return 4 * ((zz - yy) & 3) + yy

    def uv_of_member(g):
        yy, zz = g & 3, g >> 2
        return jnp.where(first, yy, zz), jnp.where(first, zz, yy)

    def uv_of_place(q):
        yy = q & 3
        zz = (yy + (q >> 2)) & 3
        return jnp.where(first, yy, zz), jnp.where(first, zz, yy)

    place = jnp.int32(0)
    for o in range(BLOCKS):
        start_ref[o] = place
        for s in range(SLOTS):

            @pl.when(s < count_ref[o])
            def _():
                owner_ref[start_ref[o] + s] = o

        place = place + count_ref[o]

    for k in range(4):
        q = place_at(u, (v + k) & 3)
        block = order_ref[q]
        bu, bv = uv_of_member(block)
        out[GRAD_PICK + k] = (u - bu) & 3
        ou, ov = uv_of_member(owner_ref[q])
        out[ROOT_PICK + k] = (u - ou) & 3
        if k == 0:
            out[GRAD_LAST] = (v - bv) & 3
            out[ROOT_LAST] = (v - ov) & 3
    my_start, my_count = start_ref[me], count_ref[me]
    slot_u = []
    for s in range(SLOTS):
        q = jnp.minimum(my_start + s, BLOCKS - 1)
        su, sv = uv_of_place(q)
        slot_u.append(su)
        out[TERM_LAST + s] = (v - sv) & 3
        out[SLOT_LIVE + s] = (s < my_count).astype(jnp.int32)
        near, far = (u - su) & 3, (v - sv) & 3
        same = ((2 * x + c) >> 2) == c
        out[SLOT_FROM + s] = jnp.where(s < my_count, jnp.where(same, far, 4 + near), 8)
        out[SLOT_ROW + s] = jnp.where(same, near, far)
    for k in range(4):
        far = (u + k) & 3
        chosen = jnp.int32(0)
        for s in range(SLOTS):
            chosen = jnp.where((s < my_count) & (slot_u[s] == far), s, chosen)
        out[SLOT_PICK + k] = chosen
        far = (v + k) & 3
        member = jnp.where(first, 4 * far + u, 4 * u + far)
        chosen = jnp.int32(0)
        for s in range(SLOTS):
            fu, fv = uv_of_place(start_ref[member] + s)
            chosen = jnp.where((s < count_ref[member]) & (fv == v), (u - fu) & 3, chosen)
        out[TERM_PICK + k] = chosen
    for k in range(4):
        for j in range(4):
            out[LANDING + k * 4 + j] = order_ref[place_at((u - j) & 3, (v - k) & 3)]
            out[LANDING + 16 + k * 4 + j] = order_ref[place_at((u - k) & 3, (v - j) & 3)]


def choices(block_order, owner_count):
    return pl.pallas_call(
        choice_kernel,
        out_shape=jax.ShapeDtypeStruct((CHOICES,), jnp.int32),
        in_specs=[SMEM, SMEM],
        out_specs=SMEM,
        scratch_shapes=[pltpu.SMEM((BLOCKS,), jnp.int32), pltpu.SMEM((BLOCKS,), jnp.int32)],
        cost_estimate=pl.CostEstimate(flops=0, bytes_accessed=4 << 20, transcendentals=0),
        name="choices",
    )(block_order, owner_count)


def cost(flops, *arrays):
    moved = sum(a.size * a.dtype.itemsize for a in arrays)
    return pl.CostEstimate(flops=flops, bytes_accessed=moved, transcendentals=0)


def small_call(body, outs, name, *args, aliases=None, flops=0, scratch=()):
    return pl.pallas_call(
        body,
        out_shape=outs,
        in_specs=[SMEM if a.dtype == jnp.int32 else VMEM for a in args],
        out_specs=jax.tree.map(lambda _: VMEM, outs),
        scratch_shapes=scratch,
        input_output_aliases=aliases or {},
        compiler_params=pltpu.CompilerParams(vmem_limit_bytes=12 << 20),
        cost_estimate=cost(flops, *args, *jax.tree.leaves(outs)),
        name=name,
    )(*args)


def copy_chosen(index, options, out, at):
    for n, option in enumerate(options):

        @pl.when(index == n)
        def _():
            out[...] = option[at]


def pair_kernel(mine, theirs, own, *sends):
    x, c, _, _ = position()
    for k in range(4):
        at = pl.ds(pl.multiple_of(c * HALF + ((x + k) & 3) * ROWS, ROWS), ROWS)
        both = mine[at, :].astype(wide_type) + theirs[at, :].astype(wide_type)
        if k == 0:
            own[...] = both
        else:
            sends[k - 1][...] = both.astype(half_type)


def pack_kernel(spot, left, right, moment, *outs):
    for k, out in enumerate(outs):
        slot = spot[SLOT_PICK + k]
        out[0] = left[slot].astype(half_type)
        out[1] = right[slot].astype(half_type)
        out[2] = moment[slot].astype(half_type)


def total_kernel(own, a, c, b, *packs):
    total = own[...] + a[...].astype(wide_type)
    total = total + b[...].astype(wide_type)
    total = (total + c[...].astype(wide_type)).astype(half_type)
    for out in packs[4:]:
        out[3] = total


def turn_kernel(spot, a, b, d, c, *outs):
    for k, out in enumerate(outs):
        copy_chosen(spot[ROOT_PICK + k], (a, b, c, d), out.at[:3], pl.ds(0, 3))
        copy_chosen(spot[GRAD_PICK + k], (a, b, c, d), out.at[3:], pl.ds(3, 1))


def here_kernel(spot, a, b, d, c, out):
    copy_chosen(spot[ROOT_LAST], (a, b, c, d), out.at[:3], pl.ds(0, 3))
    copy_chosen(spot[GRAD_LAST], (a, b, c, d), out.at[3:], pl.ds(3, 1))


def line_kernel(*refs):
    out = refs[4]
    x = position()[0]
    for n, k in enumerate((0, 2, 3, 1)):
        out[(x - k) & 3] = refs[n][...]


def line_up(got, name):
    shape = jax.ShapeDtypeStruct((4,) + got[0].shape, got[0].dtype)
    return small_call(line_kernel, shape, name, *got)


def step_kernel(mine, other, out, grad, full, held):
    x, c, _, _ = position()
    for n in range(X):
        for core, source in ((c, mine), (1 - c, other)):
            rows = pl.ds(pl.multiple_of((2 * n + core) * ROWS, ROWS), ROWS)
            for which in range(3):
                full[which, rows, :] = source[n, which]
            grad[pl.ds(pl.multiple_of(core * HALF + n * ROWS, ROWS), ROWS), :] = source[n, 3]
    g = grad[...]
    wide = g.astype(wide_type)
    grad_square = jnp.sum(wide * wide)
    precond = jnp.dot(full[0], g, preferred_element_type=wide_type).astype(half_type)
    held[...] = jnp.dot(precond, full[1], preferred_element_type=wide_type)
    dir_square = jnp.sum(held[...] * held[...])
    entries = float(BS * BS)
    top = jnp.sqrt(jnp.full((1, BS), grad_square / entries, wide_type))
    graft = top / jnp.sqrt(jnp.full((1, BS), dir_square / entries + epsilon, wide_type))
    half = pl.ds(pl.multiple_of(c * HALF, HALF), HALF)
    fresh = decay_moment * full[2, half, :].astype(wide_type) + graft * held[half, :]
    out[:HALF, :] = fresh.astype(half_type)
    rows = grad[pl.ds(pl.multiple_of((2 * x + c) * ROWS, ROWS), ROWS), :]
    out[HALF : HALF + ROWS, :] = lax.dot_general(
        rows, g, (((1,), (1,)), ((), ())), preferred_element_type=wide_type
    ).astype(half_type)
    columns = grad[:, pl.ds(pl.multiple_of(x * 2 * ROWS, 2 * ROWS), 2 * ROWS)]
    held[: 2 * ROWS, :] = lax.dot_general(
        columns, g, (((0,), (0,)), ((), ())), preferred_element_type=wide_type
    )
    term = held[pl.ds(pl.multiple_of(c * ROWS, ROWS), ROWS), :]
    out[HALF + ROWS :, :] = term.astype(half_type)


def near_kernel(spot, a, c, d, b, near, ahead, back):
    sources = (a, b, c, d)
    for out, first in ((near, 0), (ahead, ROWS), (back, 0)):
        for j, source in enumerate(sources):
            out[first + j * HALF : first + (j + 1) * HALF, :] = source[:HALF, :]
    both, left, right = pl.ds(HALF, 2 * ROWS), pl.ds(HALF, ROWS), pl.ds(HALF + ROWS, ROWS)
    copy_chosen(spot[TERM_PICK], sources, near.at[NEAR:], both)
    copy_chosen(spot[TERM_PICK + 1], sources, ahead.at[NEAR + ROWS :], both)
    copy_chosen(spot[TERM_PICK + 3], sources, back.at[NEAR + ROWS :], both)
    copy_chosen(spot[TERM_PICK + 2], sources, ahead.at[:ROWS], left)
    copy_chosen(spot[TERM_PICK + 2], sources, back.at[NEAR : NEAR + ROWS], right)


def placed_copies(spot, sources, out, sems):
    _, c, _, _ = position()
    copies = []
    for which, first, count, skip, source in sources:
        half = c if which < 4 else 1 - c
        rows = pl.ds(pl.multiple_of(half * HALF, HALF), HALF)
        for j in range(count):
            copies.append(
                pltpu.make_async_copy(
                    source.at[pl.ds(skip + j * HALF, HALF), :],
                    out.at[spot[LANDING + which * 4 + first + j], rows, :],
                    sems.at[len(copies)],
                )
            )
    return copies


def place_kernel(which, spot, *refs):
    mine, other, out, sems = refs[-4:]
    skip = ROWS if which == 1 else 0
    sources = ((which, 0, 4, skip, mine), (which + 4, 0, 4, skip, other))
    copies = placed_copies(spot, sources, out, sems)
    for copy in copies:
        copy.start()
    for copy in copies:
        copy.wait()


def place(which, spot, begun, mine, other):
    given = [mine, other] if begun is None else [begun, mine, other]
    out = jax.ShapeDtypeStruct((BLOCKS, BS, BS), half_type)
    return pl.pallas_call(
        functools.partial(place_kernel, which),
        out_shape=out,
        in_specs=[SMEM] + [ANY] * (len(given) - 2) + [VMEM] * 2,
        out_specs=ANY,
        scratch_shapes=[pltpu.SemaphoreType.DMA((8,))],
        input_output_aliases={} if begun is None else {1: 0},
        compiler_params=pltpu.CompilerParams(vmem_limit_bytes=4 << 20),
        cost_estimate=cost(0, mine, other, mine, other),
        name="place",
    )(spot, *given)


def finish_kernel(spot, begun, moment, *refs):
    del begun
    whole, halves, (out, out_moment, sems) = refs[:6], refs[6:10], refs[10:]
    near, near_other, one, one_other, three, three_other = whole
    low, high, low_other, high_other = halves
    sources = ((2, 0, 2, ROWS, low), (2, 2, 2, 0, high))
    sources += ((6, 0, 2, ROWS, low_other), (6, 2, 2, 0, high_other))
    copies = placed_copies(spot, sources, out, sems)
    for copy in copies:
        copy.start()
    x, c, _, _ = position()
    in_half = ((2 * x + c) & 3) * ROWS
    for s in range(SLOTS):
        out_moment[s] = moment[s]
        which, place = spot[SLOT_FROM + s], spot[SLOT_ROW + s]

        def take(here, source, first, skip=0):
            @pl.when(here)
            def _():
                at = pl.ds(pl.multiple_of(skip + (place - first) * HALF + in_half, ROWS), ROWS)
                out_moment[s] = source[at, :].astype(wide_type)

        take(which == 0, near, 0)
        take(which == 1, one, 0, ROWS)
        take(which == 3, three, 0)
        take(which == 4, near_other, 0)
        take(which == 5, one_other, 0, ROWS)
        take(which == 7, three_other, 0)
        take((which == 2) & (place < 2), low, 0, ROWS)
        take((which == 2) & (place >= 2), high, 2)
        take((which == 6) & (place < 2), low_other, 0, ROWS)
        take((which == 6) & (place >= 2), high_other, 2)
    for copy in copies:
        copy.wait()


def stats_kernel(spot, left, right, near, one, low, high, three, out_left, out_right):
    last = NEAR + ROWS
    terms = (
        (near.at[NEAR : NEAR + ROWS], near.at[NEAR + ROWS :]),
        (one.at[last : last + ROWS], one.at[last + ROWS :]),
        (low.at[:ROWS], high.at[2 * HALF :]),
        (three.at[last : last + ROWS], three.at[last + ROWS :]),
    )
    for s in range(SLOTS):
        out_left[s] = left[s]
        out_right[s] = right[s]
        for n, (left_term, right_term) in enumerate(terms):

            @pl.when((spot[SLOT_LIVE + s] == 1) & (spot[TERM_LAST + s] == n))
            def _():
                for old, out, term in ((left, out_left, left_term), (right, out_right, right_term)):
                    new = term[...].astype(wide_type)
                    out[s] = decay_stats * old[s] + (1.0 - decay_stats) * new


def local(
    gradients, block_order, owner_count, stat_left, stat_right, root_left, root_right, momentum
):
    chunk_type = jax.ShapeDtypeStruct((ROWS, BS), half_type)
    pack_type = jax.ShapeDtypeStruct((4, ROWS, BS), half_type)
    stat_type = jax.ShapeDtypeStruct((SLOTS, ROWS, BS), wide_type)
    hold = lax.optimization_barrier

    mine = gradients[0, 0]
    theirs = to_core(mine)
    spot, theirs = hold((choices(block_order, owner_count), theirs))
    own, *sends = small_call(
        pair_kernel,
        [jax.ShapeDtypeStruct((ROWS, BS), wide_type)] + [chunk_type] * 3,
        "pair",
        mine,
        theirs,
    )
    sends, left, right, moment = hold((sends, root_left[0], root_right[0], momentum[0]))
    packs = small_call(pack_kernel, [pack_type] * 4, "packs", spot, left, right, moment)
    got = along(to_x, [own] + sends)

    packs = small_call(
        total_kernel, [pack_type] * 4, "total", *got, *packs, aliases={4: 0, 5: 1, 6: 2, 7: 3}
    )
    row = along(to_u, packs)
    column = along(to_v, small_call(turn_kernel, [pack_type] * 4, "turn", spot, *row))
    pack = small_call(here_kernel, pack_type, "here", spot, *column)
    full = line_up(along(to_x, [pack] * 4, (2, 3, 1)), "line")
    send = small_call(
        step_kernel,
        jax.ShapeDtypeStruct((HALF + 2 * ROWS, BS), half_type),
        "step",
        full,
        to_core(full),
        flops=6 * BS**3,
        scratch=[
            pltpu.VMEM((BS, BS), half_type),
            pltpu.VMEM((3, BS, BS), half_type),
            pltpu.VMEM((BS, BS), wide_type),
        ],
    )

    row = along(to_u, [send] * 4, (2, 3, 1))
    near_type = jax.ShapeDtypeStruct((NEAR + 2 * ROWS, BS), half_type)
    sent_type = jax.ShapeDtypeStruct((NEAR + 3 * ROWS, BS), half_type)
    near, ahead, back = small_call(
        near_kernel, [near_type, sent_type, sent_type], "near", spot, *row
    )
    one, three = to_v(ahead, 1), to_v(back, 3)
    near_other = to_core(near)
    low = to_v(one[: ROWS + 2 * HALF], 1)
    high = to_v(three[2 * HALF : NEAR + ROWS], 3)
    one_other, three_other = to_core(one), to_core(three)
    begun = place(0, spot, None, near, near_other)
    begun = place(1, spot, begun, one, one_other)
    begun = place(3, spot, begun, three, three_other)
    low, high, begun = hold((low, high, begun))
    left_stats, right_stats = small_call(
        stats_kernel,
        [stat_type] * 2,
        "stats",
        spot,
        stat_left[0],
        stat_right[0],
        near,
        one,
        low,
        high,
        three,
    )
    given = [near, near_other, one, one_other, three, three_other]
    given += [low, high, to_core(low), to_core(high)]
    update_blocks, new_momentum = pl.pallas_call(
        finish_kernel,
        out_shape=[jax.ShapeDtypeStruct((BLOCKS, BS, BS), half_type), stat_type],
        in_specs=[SMEM, ANY] + [VMEM] * (1 + len(given)),
        out_specs=[ANY, VMEM],
        scratch_shapes=[pltpu.SemaphoreType.DMA((8,))],
        input_output_aliases={1: 0},
        compiler_params=pltpu.CompilerParams(vmem_limit_bytes=16 << 20),
        cost_estimate=cost(0, *given),
        name="finish",
    )(spot, begun, momentum[0], *given)
    return (update_blocks, left_stats[None], right_stats[None], new_momentum[None])


def solution(mesh):
    placed = (
        P("dp", "group", None, None),
        P(),
        P(),
        P("group", None, "dp", None),
        P("group", None, "dp", None),
        P("group", None, "dp", None),
        P("group", None, "dp", None),
        P("group", None, "dp", None),
    )
    return jax.shard_map(
        local,
        mesh=mesh,
        in_specs=placed,
        out_specs=(
            P(),
            P("group", None, "dp", None),
            P("group", None, "dp", None),
            P("group", None, "dp", None),
        ),
        check_vma=False,
    )
```

```python
import functools

import jax
import jax.numpy as jnp
from jax import lax
from jax.experimental import pallas as pl
from jax.experimental.pallas import tpu as pltpu
from jax.sharding import PartitionSpec as P

decay_stats = 0.95
decay_moment = 0.9
epsilon = 1e-06

AXES = ("dp", "group")
X, CORES, SIDE, SLOTS = 4, 2, 4, 3
BLOCKS = SIDE * SIDE
BS = 512
ROWS = BS // (X * CORES)
HALF = BS // CORES
NEAR = SIDE * HALF
half_type = jnp.bfloat16
wide_type = jnp.float32

SMEM = pl.BlockSpec(memory_space=pltpu.SMEM)
VMEM = pl.BlockSpec(memory_space=pltpu.VMEM)
ANY = pl.BlockSpec(memory_space=pl.ANY)

GRAD_PICK, GRAD_LAST, ROOT_PICK, ROOT_LAST, TERM_PICK, TILES = 0, 4, 5, 9, 10, 14
SLOT_PICK, TERM_LAST, SLOT_LIVE, SLOT_FROM, SLOT_ROW = 14, 18, 21, 24, 27
LANDING = 30
CHOICES = LANDING + 32


def permute(value, target):
    pairs = []
    for x in range(X):
        for c in range(CORES):
            for z in range(SIDE):
                for y in range(SIDE):
                    tx, tc, tz, ty = target(x, c, z, y)
                    pairs.append(
                        ((x * 2 + c) * 16 + z * 4 + y, ((tx % 4) * 2 + tc) * 16 + (tz % 4) * 4 + ty % 4)
                    )
    return lax.ppermute(value, AXES, pairs)


def to_core(value):
    return permute(value, lambda x, c, z, y: (x, 1 - c, z, y))


def to_x(value, k):
    return permute(value, lambda x, c, z, y: (x + k, c, z, y))


def to_u(value, k):
    return permute(value, lambda x, c, z, y: (x, c, z, y + k) if c == 0 else (x, c, z + k, y))


def to_v(value, k):
    return permute(value, lambda x, c, z, y: (x, c, z + k, y) if c == 0 else (x, c, z, y + k))


def along(send, values, shifts=(1, 3, 2)):
    return [values[0]] + [send(values[k], k) for k in shifts]


def position():
    dp, me = lax.axis_index("dp"), lax.axis_index("group")
    return dp >> 1, dp & 1, me >> 2, me & 3


def choice_kernel(order_ref, count_ref, out, tiles, start_ref, owner_ref):
    x, c, z, y = position()
    me = z * 4 + y
    first = c == 0
    u, v = jnp.where(first, y, z), jnp.where(first, z, y)

    def place_at(uu, vv):
        yy, zz = jnp.where(first, uu, vv), jnp.where(first, vv, uu)
        return 4 * ((zz - yy) & 3) + yy

    def uv_of_member(g):
        yy, zz = g & 3, g >> 2
        return jnp.where(first, yy, zz), jnp.where(first, zz, yy)

    def uv_of_place(q):
        yy = q & 3
        zz = (yy + (q >> 2)) & 3
        return jnp.where(first, yy, zz), jnp.where(first, zz, yy)

    place = jnp.int32(0)
    for o in range(BLOCKS):
        start_ref[o] = place
        for s in range(SLOTS):

            @pl.when(s < count_ref[o])
            def _():
                owner_ref[start_ref[o] + s] = o

        place = place + count_ref[o]

    for k in range(4):
        q = place_at(u, (v + k) & 3)
        block = order_ref[q]
        bu, bv = uv_of_member(block)
        out[GRAD_PICK + k] = (u - bu) & 3
        ou, ov = uv_of_member(owner_ref[q])
        out[ROOT_PICK + k] = (u - ou) & 3
        if k == 0:
            out[GRAD_LAST] = (v - bv) & 3
            out[ROOT_LAST] = (v - ov) & 3
    my_start, my_count = start_ref[me], count_ref[me]
    slot_u = []
    for s in range(SLOTS):
        q = jnp.minimum(my_start + s, BLOCKS - 1)
        su, sv = uv_of_place(q)
        slot_u.append(su)
        out[TERM_LAST + s] = (v - sv) & 3
        out[SLOT_LIVE + s] = (s < my_count).astype(jnp.int32)
        out[SLOT_FROM + s] = jnp.where(s < my_count, (v - sv) & 3, 8)
        out[SLOT_ROW + s] = (u - su) & 3
    for k in range(4):
        far = (u + k) & 3
        chosen = jnp.int32(0)
        for s in range(SLOTS):
            chosen = jnp.where((s < my_count) & (slot_u[s] == far), s, chosen)
        out[SLOT_PICK + k] = chosen
        far = (v + k) & 3
        member = jnp.where(first, 4 * far + u, 4 * u + far)
        chosen = jnp.int32(0)
        for s in range(SLOTS):
            fu, fv = uv_of_place(start_ref[member] + s)
            chosen = jnp.where((s < count_ref[member]) & (fv == v), (u - fu) & 3, chosen)
        out[TERM_PICK + k] = chosen
    for k in range(4):
        for j in range(4):
            out[LANDING + k * 4 + j] = order_ref[place_at((u - j) & 3, (v - k) & 3)]
            out[LANDING + 16 + k * 4 + j] = order_ref[place_at((u - k) & 3, (v - j) & 3)]
    for n in range(TILES):
        tiles[n] = jnp.full((16, BS), out[n].astype(wide_type), wide_type).astype(half_type)


def choices(block_order, owner_count):
    return pl.pallas_call(
        choice_kernel,
        out_shape=[
            jax.ShapeDtypeStruct((CHOICES,), jnp.int32),
            jax.ShapeDtypeStruct((TILES, 16, BS), half_type),
        ],
        in_specs=[SMEM, SMEM],
        out_specs=[SMEM, VMEM],
        scratch_shapes=[pltpu.SMEM((BLOCKS,), jnp.int32), pltpu.SMEM((BLOCKS,), jnp.int32)],
        cost_estimate=pl.CostEstimate(flops=0, bytes_accessed=4 << 20, transcendentals=0),
        name="choices",
    )(block_order, owner_count)


def cost(flops, *arrays):
    moved = sum(a.size * a.dtype.itemsize for a in arrays)
    return pl.CostEstimate(flops=flops, bytes_accessed=moved, transcendentals=0)


def small_call(body, outs, name, *args, aliases=None, flops=0, scratch=()):
    return pl.pallas_call(
        body,
        out_shape=outs,
        in_specs=[SMEM if a.dtype == jnp.int32 else VMEM for a in args],
        out_specs=jax.tree.map(lambda _: VMEM, outs),
        scratch_shapes=scratch,
        input_output_aliases=aliases or {},
        compiler_params=pltpu.CompilerParams(vmem_limit_bytes=12 << 20),
        cost_estimate=cost(flops, *args, *jax.tree.leaves(outs)),
        name=name,
    )(*args)


def blend(choice, options):
    rows = options[0].shape[0]
    parts = [option.reshape(rows // 16, 16, BS) for option in options]
    out = parts[3]
    for n in (2, 1, 0):
        out = jnp.where(choice[None] == n, parts[n], out)
    return out.reshape(rows, BS)


def half_kernel(given, out):
    c = position()[1]
    out[...] = given[pl.ds(pl.multiple_of(c * HALF, HALF), HALF), :]


def pair_kernel(mine, theirs, own, *sends):
    x, c, _, _ = position()
    for k in range(4):
        row = ((x + k) & 3) * ROWS
        at = pl.ds(pl.multiple_of(row, ROWS), ROWS)
        far = pl.ds(pl.multiple_of(c * HALF + row, ROWS), ROWS)
        both = mine[at, :].astype(wide_type) + theirs[far, :].astype(wide_type)
        if k == 0:
            own[...] = both
        else:
            sends[k - 1][...] = both.astype(half_type)


def pack_kernel(spot, left, right, moment, *outs):
    for k, out in enumerate(outs):
        slot = spot[SLOT_PICK + k]
        out[0] = left[slot].astype(half_type)
        out[1] = right[slot].astype(half_type)
        out[2] = moment[slot].astype(half_type)


def total_kernel(own, a, c, b, *packs):
    total = own[...] + a[...].astype(wide_type)
    total = total + b[...].astype(wide_type)
    total = (total + c[...].astype(wide_type)).astype(half_type)
    for out in packs[4:]:
        out[3] = total


def turn_kernel(tiles, a, b, d, c, *outs):
    for n in range(4):
        options = [source[n] for source in (a, b, c, d)]
        base = GRAD_PICK if n == 3 else ROOT_PICK
        for k, out in enumerate(outs):
            out[n] = blend(tiles[base + k], options)


def here_kernel(tiles, a, b, d, c, out):
    for n in range(4):
        options = [source[n] for source in (a, b, c, d)]
        out[n] = blend(tiles[GRAD_LAST if n == 3 else ROOT_LAST], options)


def line_kernel(*refs):
    shared, moment = refs[4:]
    x = position()[0]
    for i, k in enumerate((0, 2, 3, 1)):
        n = (x - k) & 3
        shared[n, 0] = refs[i][0]
        shared[n, 1] = refs[i][1]
        shared[n, 2] = refs[i][3]
        moment[n] = refs[i][2]


def step_kernel(mine, moment, other, out, grad, full, held):
    x, c, _, _ = position()
    for n in range(X):
        for core, source in ((c, mine), (1 - c, other)):
            rows = pl.ds(pl.multiple_of((2 * n + core) * ROWS, ROWS), ROWS)
            for which in range(2):
                full[which, rows, :] = source[n, which]
            grad[pl.ds(pl.multiple_of(core * HALF + n * ROWS, ROWS), ROWS), :] = source[n, 2]
    g = grad[...]
    wide = g.astype(wide_type)
    grad_square = jnp.sum(wide * wide)
    precond = jnp.dot(full[0], g, preferred_element_type=wide_type).astype(half_type)
    held[...] = jnp.dot(precond, full[1], preferred_element_type=wide_type)
    dir_square = jnp.sum(held[...] * held[...])
    entries = float(BS * BS)
    top = jnp.sqrt(jnp.full((1, BS), grad_square / entries, wide_type))
    graft = top / jnp.sqrt(jnp.full((1, BS), dir_square / entries + epsilon, wide_type))
    for n in range(X):
        rows = pl.ds(pl.multiple_of((2 * n + c) * ROWS, ROWS), ROWS)
        fresh = decay_moment * moment[n].astype(wide_type) + graft * held[rows, :]
        out[n] = fresh.astype(half_type)
    rows = grad[pl.ds(pl.multiple_of((2 * x + c) * ROWS, ROWS), ROWS), :]
    out[4] = lax.dot_general(
        rows, g, (((1,), (1,)), ((), ())), preferred_element_type=wide_type
    ).astype(half_type)
    columns = grad[:, pl.ds(pl.multiple_of(x * 2 * ROWS, 2 * ROWS), 2 * ROWS)]
    held[: 2 * ROWS, :] = lax.dot_general(
        columns, g, (((0,), (0,)), ((), ())), preferred_element_type=wide_type
    )
    out[5] = held[pl.ds(pl.multiple_of(c * ROWS, ROWS), ROWS), :].astype(half_type)


def near_kernel(tiles, a, c, d, b, near, ahead, back):
    sources = (a, b, c, d)
    for out, first in ((near, 0), (ahead, 1), (back, 0)):
        for j, source in enumerate(sources):
            out[first + j * 4 : first + j * 4 + 4] = source[:4]
    left = [source[4] for source in sources]
    right = [source[5] for source in sources]
    for k, out, first in ((0, near, 16), (1, ahead, 17), (3, back, 17)):
        out[first] = blend(tiles[TERM_PICK + k], left)
        out[first + 1] = blend(tiles[TERM_PICK + k], right)
    ahead[0] = blend(tiles[TERM_PICK + 2], left)
    back[16] = blend(tiles[TERM_PICK + 2], right)


def placed_copies(spot, sources, out, sems):
    _, c, _, _ = position()
    copies = []
    for which, first, count, skip, source in sources:
        half = c if which < 4 else 1 - c
        for j in range(count):
            copies.append(
                pltpu.make_async_copy(
                    source.at[pl.ds(skip + j * 4, 4)],
                    out.at[spot[LANDING + which * 4 + first + j], :, half],
                    sems.at[len(copies)],
                )
            )
    return copies


def place_kernel(which, spot, *refs):
    mine, other, out, sems = refs[-4:]
    skip = 1 if which == 1 else 0
    sources = ((which, 0, 4, skip, mine), (which + 4, 0, 4, skip, other))
    copies = placed_copies(spot, sources, out, sems)
    for copy in copies:
        copy.start()
    for copy in copies:
        copy.wait()


def place(which, spot, begun, mine, other):
    given = [mine, other] if begun is None else [begun, mine, other]
    return pl.pallas_call(
        functools.partial(place_kernel, which),
        out_shape=jax.ShapeDtypeStruct((BLOCKS, X, CORES, ROWS, BS), half_type),
        in_specs=[SMEM] + [ANY] * (len(given) - 2) + [VMEM] * 2,
        out_specs=ANY,
        scratch_shapes=[pltpu.SemaphoreType.DMA((8,))],
        input_output_aliases={} if begun is None else {1: 0},
        compiler_params=pltpu.CompilerParams(vmem_limit_bytes=4 << 20),
        cost_estimate=cost(0, mine, other, mine, other),
        name="place",
    )(spot, *given)


def finish_kernel(spot, begun, moment, near, one, three, low, high, low_other, high_other, *refs):
    del begun
    out, out_moment, fresh, sems, more = refs
    sources = ((2, 0, 2, 1, low), (2, 2, 2, 0, high))
    sources += ((6, 0, 2, 1, low_other), (6, 2, 2, 0, high_other))
    copies = placed_copies(spot, sources, out, sems)
    for copy in copies:
        copy.start()
    x = position()[0]
    parts = ((0, 0, 4, 0, near), (1, 0, 4, 1, one), (3, 0, 4, 0, three)) + sources[:2]
    for s in range(SLOTS):
        fresh[s] = moment[s]
        came, place = spot[SLOT_FROM + s], spot[SLOT_ROW + s]
        for which, first, count, skip, source in parts:

            @pl.when((came == which) & (place >= first) & (place < first + count))
            def _():
                fresh[s] = source[skip + (place - first) * 4 + x].astype(wide_type)

        copy = pltpu.make_async_copy(fresh.at[s], out_moment.at[s], more.at[s])
        copy.start()
        copies.append(copy)
    for copy in copies:
        copy.wait()


def stats_kernel(spot, left, right, near, one, low, high, three, out_left, out_right):
    terms = ((near, 16, near, 17), (one, 17, one, 18), (low, 0, high, 8), (three, 17, three, 18))
    for s in range(SLOTS):
        out_left[s] = left[s]
        out_right[s] = right[s]
        for n, (left_from, m, right_from, r) in enumerate(terms):

            @pl.when((spot[SLOT_LIVE + s] == 1) & (spot[TERM_LAST + s] == n))
            def _():
                new = left_from[m].astype(wide_type)
                out_left[s] = decay_stats * left[s] + (1.0 - decay_stats) * new
                new = right_from[r].astype(wide_type)
                out_right[s] = decay_stats * right[s] + (1.0 - decay_stats) * new


def local(
    gradients, block_order, owner_count, stat_left, stat_right, root_left, root_right, momentum
):
    chunk_type = jax.ShapeDtypeStruct((ROWS, BS), half_type)
    pack_type = jax.ShapeDtypeStruct((4, ROWS, BS), half_type)
    stat_type = jax.ShapeDtypeStruct((SLOTS, ROWS, BS), wide_type)
    hold = lax.optimization_barrier

    mine = gradients[0, 0]
    theirs = to_core(mine)
    mine = small_call(half_kernel, jax.ShapeDtypeStruct((HALF, BS), half_type), "half", mine)
    mine, theirs = hold((mine, theirs))
    own, *sends = small_call(
        pair_kernel,
        [jax.ShapeDtypeStruct((ROWS, BS), wide_type)] + [chunk_type] * 3,
        "pair",
        mine,
        theirs,
    )
    sends, order, count, left, right, moment = hold(
        (sends, block_order, owner_count, root_left[0], root_right[0], momentum[0])
    )
    spot, tiles = choices(order, count)
    packs = small_call(pack_kernel, [pack_type] * 4, "packs", spot, left, right, moment)
    got = along(to_x, [own] + sends)

    packs = small_call(
        total_kernel, [pack_type] * 4, "total", *got, *packs, aliases={4: 0, 5: 1, 6: 2, 7: 3}
    )
    row = along(to_u, packs)
    column = along(to_v, small_call(turn_kernel, [pack_type] * 4, "turn", tiles, *row))
    pack = small_call(here_kernel, pack_type, "here", tiles, *column)
    shared, moment = small_call(
        line_kernel,
        [
            jax.ShapeDtypeStruct((X, 3, ROWS, BS), half_type),
            jax.ShapeDtypeStruct((X, ROWS, BS), half_type),
        ],
        "line",
        *along(to_x, [pack] * 4, (2, 3, 1)),
    )
    send = small_call(
        step_kernel,
        jax.ShapeDtypeStruct((6, ROWS, BS), half_type),
        "step",
        shared,
        moment,
        to_core(shared),
        flops=6 * BS**3,
        scratch=[
            pltpu.VMEM((BS, BS), half_type),
            pltpu.VMEM((2, BS, BS), half_type),
            pltpu.VMEM((BS, BS), wide_type),
        ],
    )

    row = along(to_u, [send] * 4, (2, 3, 1))
    near_type = jax.ShapeDtypeStruct((18, ROWS, BS), half_type)
    sent_type = jax.ShapeDtypeStruct((19, ROWS, BS), half_type)
    near, ahead, back = small_call(
        near_kernel, [near_type, sent_type, sent_type], "near", tiles, *row
    )
    one, three = to_v(ahead, 1), to_v(back, 3)
    near_other = to_core(near)
    low = to_v(one[:9], 1)
    high = to_v(three[8:17], 3)
    one_other, three_other = to_core(one), to_core(three)
    begun = place(0, spot, None, near, near_other)
    begun = place(1, spot, begun, one, one_other)
    begun = place(3, spot, begun, three, three_other)
    low, high, begun = hold((low, high, begun))
    left_stats, right_stats = small_call(
        stats_kernel,
        [stat_type] * 2,
        "stats",
        spot,
        stat_left[0],
        stat_right[0],
        near,
        one,
        low,
        high,
        three,
    )
    given = [near, one, three, low, high, to_core(low), to_core(high)]
    update_blocks, new_momentum = pl.pallas_call(
        finish_kernel,
        out_shape=[jax.ShapeDtypeStruct(begun.shape, half_type), stat_type],
        in_specs=[SMEM, ANY] + [VMEM] * (1 + len(given)),
        out_specs=[ANY, ANY],
        scratch_shapes=[
            pltpu.VMEM((SLOTS, ROWS, BS), wide_type),
            pltpu.SemaphoreType.DMA((8,)),
            pltpu.SemaphoreType.DMA((SLOTS,)),
        ],
        input_output_aliases={1: 0},
        compiler_params=pltpu.CompilerParams(vmem_limit_bytes=16 << 20),
        cost_estimate=cost(0, *given),
        name="finish",
    )(spot, begun, momentum[0], *given)
    update_blocks = update_blocks.reshape(BLOCKS, BS, BS)
    return (update_blocks, left_stats[None], right_stats[None], new_momentum[None])


def solution(mesh):
    placed = (
        P("dp", "group", None, None),
        P(),
        P(),
        P("group", None, "dp", None),
        P("group", None, "dp", None),
        P("group", None, "dp", None),
        P("group", None, "dp", None),
        P("group", None, "dp", None),
    )
    return jax.shard_map(
        local,
        mesh=mesh,
        in_specs=placed,
        out_specs=(
            P(),
            P("group", None, "dp", None),
            P("group", None, "dp", None),
            P("group", None, "dp", None),
        ),
        check_vma=False,
    )
```

```python
import functools

import jax
import jax.numpy as jnp
from jax import lax
from jax.experimental import pallas as pl
from jax.experimental.pallas import tpu as pltpu
from jax.sharding import PartitionSpec as P

decay_stats = 0.95
decay_moment = 0.9
epsilon = 1e-06

AXES = ("dp", "group")
X, CORES, SIDE, SLOTS = 4, 2, 4, 3
BLOCKS = SIDE * SIDE
BS = 512
ROWS = BS // (X * CORES)
HALF = BS // CORES
NEAR = SIDE * HALF
half_type = jnp.bfloat16
wide_type = jnp.float32

SMEM = pl.BlockSpec(memory_space=pltpu.SMEM)
VMEM = pl.BlockSpec(memory_space=pltpu.VMEM)
ANY = pl.BlockSpec(memory_space=pl.ANY)

GRAD_PICK, GRAD_LAST, ROOT_PICK, ROOT_LAST, TERM_PICK, TILES = 0, 4, 5, 9, 10, 14
SLOT_PICK, TERM_LAST, SLOT_LIVE, SLOT_FROM, SLOT_ROW = 14, 18, 21, 24, 27
LANDING = 30
CHOICES = LANDING + 32


def permute(value, target):
    pairs = []
    for x in range(X):
        for c in range(CORES):
            for z in range(SIDE):
                for y in range(SIDE):
                    tx, tc, tz, ty = target(x, c, z, y)
                    pairs.append(
                        ((x * 2 + c) * 16 + z * 4 + y, ((tx % 4) * 2 + tc) * 16 + (tz % 4) * 4 + ty % 4)
                    )
    return lax.ppermute(value, AXES, pairs)


def to_core(value):
    return permute(value, lambda x, c, z, y: (x, 1 - c, z, y))


def to_x(value, k):
    return permute(value, lambda x, c, z, y: (x + k, c, z, y))


def to_u(value, k):
    return permute(value, lambda x, c, z, y: (x, c, z, y + k) if c == 0 else (x, c, z + k, y))


def to_v(value, k):
    return permute(value, lambda x, c, z, y: (x, c, z + k, y) if c == 0 else (x, c, z, y + k))


def along(send, values, shifts=(1, 3, 2)):
    return [values[0]] + [send(values[k], k) for k in shifts]


def position():
    dp, me = lax.axis_index("dp"), lax.axis_index("group")
    return dp >> 1, dp & 1, me >> 2, me & 3


def choice_kernel(order_ref, count_ref, out, tiles, start_ref, owner_ref):
    x, c, z, y = position()
    me = z * 4 + y
    first = c == 0
    u, v = jnp.where(first, y, z), jnp.where(first, z, y)

    def place_at(uu, vv):
        yy, zz = jnp.where(first, uu, vv), jnp.where(first, vv, uu)
        return 4 * ((zz - yy) & 3) + yy

    def uv_of_member(g):
        yy, zz = g & 3, g >> 2
        return jnp.where(first, yy, zz), jnp.where(first, zz, yy)

    def uv_of_place(q):
        yy = q & 3
        zz = (yy + (q >> 2)) & 3
        return jnp.where(first, yy, zz), jnp.where(first, zz, yy)

    place = jnp.int32(0)
    for o in range(BLOCKS):
        start_ref[o] = place
        for s in range(SLOTS):

            @pl.when(s < count_ref[o])
            def _():
                owner_ref[start_ref[o] + s] = o

        place = place + count_ref[o]

    for k in range(4):
        q = place_at(u, (v + k) & 3)
        block = order_ref[q]
        bu, bv = uv_of_member(block)
        out[GRAD_PICK + k] = (u - bu) & 3
        ou, ov = uv_of_member(owner_ref[q])
        out[ROOT_PICK + k] = (u - ou) & 3
        if k == 0:
            out[GRAD_LAST] = (v - bv) & 3
            out[ROOT_LAST] = (v - ov) & 3
    my_start, my_count = start_ref[me], count_ref[me]
    slot_u = []
    for s in range(SLOTS):
        q = jnp.minimum(my_start + s, BLOCKS - 1)
        su, sv = uv_of_place(q)
        slot_u.append(su)
        out[TERM_LAST + s] = (v - sv) & 3
        out[SLOT_LIVE + s] = (s < my_count).astype(jnp.int32)
        out[SLOT_FROM + s] = jnp.where(s < my_count, (v - sv) & 3, 8)
        out[SLOT_ROW + s] = (u - su) & 3
    for k in range(4):
        far = (u + k) & 3
        chosen = jnp.int32(0)
        for s in range(SLOTS):
            chosen = jnp.where((s < my_count) & (slot_u[s] == far), s, chosen)
        out[SLOT_PICK + k] = chosen
        far = (v + k) & 3
        member = jnp.where(first, 4 * far + u, 4 * u + far)
        chosen = jnp.int32(0)
        for s in range(SLOTS):
            fu, fv = uv_of_place(start_ref[member] + s)
            chosen = jnp.where((s < count_ref[member]) & (fv == v), (u - fu) & 3, chosen)
        out[TERM_PICK + k] = chosen
    for k in range(4):
        for j in range(4):
            out[LANDING + k * 4 + j] = order_ref[place_at((u - j) & 3, (v - k) & 3)]
            out[LANDING + 16 + k * 4 + j] = order_ref[place_at((u - k) & 3, (v - j) & 3)]
    for n in range(TILES):
        tiles[n] = jnp.full((16, BS), out[n].astype(wide_type), wide_type).astype(half_type)


def choices(block_order, owner_count):
    return pl.pallas_call(
        choice_kernel,
        out_shape=[
            jax.ShapeDtypeStruct((CHOICES,), jnp.int32),
            jax.ShapeDtypeStruct((TILES, 16, BS), half_type),
        ],
        in_specs=[SMEM, SMEM],
        out_specs=[SMEM, VMEM],
        scratch_shapes=[pltpu.SMEM((BLOCKS,), jnp.int32), pltpu.SMEM((BLOCKS,), jnp.int32)],
        cost_estimate=pl.CostEstimate(flops=0, bytes_accessed=4 << 20, transcendentals=0),
        name="choices",
    )(block_order, owner_count)


def cost(flops, *arrays):
    moved = sum(a.size * a.dtype.itemsize for a in arrays)
    return pl.CostEstimate(flops=flops, bytes_accessed=moved, transcendentals=0)


def small_call(body, outs, name, *args, aliases=None, flops=0, scratch=()):
    return pl.pallas_call(
        body,
        out_shape=outs,
        in_specs=[SMEM if a.dtype == jnp.int32 else VMEM for a in args],
        out_specs=jax.tree.map(lambda _: VMEM, outs),
        scratch_shapes=scratch,
        input_output_aliases=aliases or {},
        compiler_params=pltpu.CompilerParams(vmem_limit_bytes=12 << 20),
        cost_estimate=cost(flops, *args, *jax.tree.leaves(outs)),
        name=name,
    )(*args)


def blend(choice, options):
    rows = options[0].shape[0]
    parts = [option.reshape(rows // 16, 16, BS) for option in options]
    out = parts[3]
    for n in (2, 1, 0):
        out = jnp.where(choice[None] == n, parts[n], out)
    return out.reshape(rows, BS)


def half_kernel(given, out):
    c = position()[1]
    out[...] = given[pl.ds(pl.multiple_of(c * HALF, HALF), HALF), :]


def pair_kernel(mine, theirs, own, *sends):
    x, c, _, _ = position()
    for k in range(4):
        row = ((x + k) & 3) * ROWS
        at = pl.ds(pl.multiple_of(row, ROWS), ROWS)
        far = pl.ds(pl.multiple_of(c * HALF + row, ROWS), ROWS)
        both = mine[at, :].astype(wide_type) + theirs[far, :].astype(wide_type)
        if k == 0:
            own[...] = both
        else:
            sends[k - 1][...] = both.astype(half_type)


def pack_kernel(spot, left, right, moment, *outs):
    for k, out in enumerate(outs):
        slot = spot[SLOT_PICK + k]
        out[0] = left[slot].astype(half_type)
        out[1] = right[slot].astype(half_type)
        out[2] = moment[slot].astype(half_type)


def total_kernel(own, a, c, b, *packs):
    total = own[...] + a[...].astype(wide_type)
    total = total + b[...].astype(wide_type)
    total = (total + c[...].astype(wide_type)).astype(half_type)
    for out in packs[4:]:
        out[3] = total


def turn_kernel(tiles, a, c, b, d, *outs):
    for n in range(4):
        options = [source[n] for source in (a, b, c, d)]
        base = GRAD_PICK if n == 3 else ROOT_PICK
        for k, out in enumerate(outs):
            out[n] = blend(tiles[base + k], options)


def here_kernel(tiles, a, c, b, d, out):
    for n in range(4):
        options = [source[n] for source in (a, b, c, d)]
        out[n] = blend(tiles[GRAD_LAST if n == 3 else ROOT_LAST], options)


def line_kernel(*refs):
    shared, moment = refs[4:]
    x = position()[0]
    for i, k in enumerate((0, 2, 1, 3)):
        n = (x - k) & 3
        shared[n, 0] = refs[i][0]
        shared[n, 1] = refs[i][1]
        shared[n, 2] = refs[i][3]
        moment[n] = refs[i][2]


def step_kernel(mine, moment, other, out, grad, full, held):
    x, c, _, _ = position()
    for n in range(X):
        for core, source in ((c, mine), (1 - c, other)):
            rows = pl.ds(pl.multiple_of((2 * n + core) * ROWS, ROWS), ROWS)
            for which in range(2):
                full[which, rows, :] = source[n, which]
            grad[pl.ds(pl.multiple_of(core * HALF + n * ROWS, ROWS), ROWS), :] = source[n, 2]
    g = grad[...]
    wide = g.astype(wide_type)
    grad_square = jnp.sum(wide * wide)
    precond = jnp.dot(full[0], g, preferred_element_type=wide_type).astype(half_type)
    held[...] = jnp.dot(precond, full[1], preferred_element_type=wide_type)
    dir_square = jnp.sum(held[...] * held[...])
    entries = float(BS * BS)
    top = jnp.sqrt(jnp.full((1, BS), grad_square / entries, wide_type))
    graft = top / jnp.sqrt(jnp.full((1, BS), dir_square / entries + epsilon, wide_type))
    for n in range(X):
        rows = pl.ds(pl.multiple_of((2 * n + c) * ROWS, ROWS), ROWS)
        fresh = decay_moment * moment[n].astype(wide_type) + graft * held[rows, :]
        out[n] = fresh.astype(half_type)
    rows = grad[pl.ds(pl.multiple_of((2 * x + c) * ROWS, ROWS), ROWS), :]
    out[4] = lax.dot_general(
        rows, g, (((1,), (1,)), ((), ())), preferred_element_type=wide_type
    ).astype(half_type)
    columns = grad[:, pl.ds(pl.multiple_of(x * 2 * ROWS, 2 * ROWS), 2 * ROWS)]
    held[: 2 * ROWS, :] = lax.dot_general(
        columns, g, (((0,), (0,)), ((), ())), preferred_element_type=wide_type
    )
    out[5] = held[pl.ds(pl.multiple_of(c * ROWS, ROWS), ROWS), :].astype(half_type)


def near_kernel(tiles, a, c, b, d, near, ahead, back):
    sources = (a, b, c, d)
    for out, first in ((near, 0), (ahead, 1), (back, 0)):
        for j, source in enumerate(sources):
            out[first + j * 4 : first + j * 4 + 4] = source[:4]
    left = [source[4] for source in sources]
    right = [source[5] for source in sources]
    for k, out, first in ((0, near, 16), (1, ahead, 17), (3, back, 17)):
        out[first] = blend(tiles[TERM_PICK + k], left)
        out[first + 1] = blend(tiles[TERM_PICK + k], right)
    ahead[0] = blend(tiles[TERM_PICK + 2], left)
    back[16] = blend(tiles[TERM_PICK + 2], right)


def placed_copies(spot, sources, out, sems):
    _, c, _, _ = position()
    copies = []
    for which, first, count, skip, source in sources:
        half = c if which < 4 else 1 - c
        for j in range(count):
            copies.append(
                pltpu.make_async_copy(
                    source.at[pl.ds(skip + j * 4, 4)],
                    out.at[spot[LANDING + which * 4 + first + j], :, half],
                    sems.at[len(copies)],
                )
            )
    return copies


def place_kernel(which, spot, *refs):
    mine, other, out, sems = refs[-4:]
    skip = 1 if which == 1 else 0
    sources = ((which, 0, 4, skip, mine), (which + 4, 0, 4, skip, other))
    copies = placed_copies(spot, sources, out, sems)
    for copy in copies:
        copy.start()
    for copy in copies:
        copy.wait()


def place(which, spot, begun, mine, other):
    given = [mine, other] if begun is None else [begun, mine, other]
    return pl.pallas_call(
        functools.partial(place_kernel, which),
        out_shape=jax.ShapeDtypeStruct((BLOCKS, X, CORES, ROWS, BS), half_type),
        in_specs=[SMEM] + [ANY] * (len(given) - 2) + [VMEM] * 2,
        out_specs=ANY,
        scratch_shapes=[pltpu.SemaphoreType.DMA((8,))],
        input_output_aliases={} if begun is None else {1: 0},
        compiler_params=pltpu.CompilerParams(vmem_limit_bytes=4 << 20),
        cost_estimate=cost(0, mine, other, mine, other),
        name="place",
    )(spot, *given)


def owner_kernel(spot, begun, moment, left, right, near, one, three, low, high, *refs):
    del begun
    out, out_moment, out_left, out_right, fresh, new_left, new_right, sems, more = refs
    sources = ((2, 0, 2, 1, low), (2, 2, 2, 0, high))
    copies = placed_copies(spot, sources, out, sems)
    for copy in copies:
        copy.start()
    x = position()[0]
    parts = ((0, 0, 4, 0, near), (1, 0, 4, 1, one), (3, 0, 4, 0, three)) + sources
    terms = ((near, 16, near, 17), (one, 17, one, 18), (low, 0, high, 8), (three, 17, three, 18))
    for s in range(SLOTS):
        fresh[s] = moment[s]
        new_left[s] = left[s]
        new_right[s] = right[s]
        came, place = spot[SLOT_FROM + s], spot[SLOT_ROW + s]
        for which, first, count, skip, source in parts:

            @pl.when((came == which) & (place >= first) & (place < first + count))
            def _():
                fresh[s] = source[skip + (place - first) * 4 + x].astype(wide_type)

        for n, (left_from, m, right_from, r) in enumerate(terms):

            @pl.when((spot[SLOT_LIVE + s] == 1) & (spot[TERM_LAST + s] == n))
            def _():
                term = left_from[m].astype(wide_type)
                new_left[s] = decay_stats * left[s] + (1.0 - decay_stats) * term
                term = right_from[r].astype(wide_type)
                new_right[s] = decay_stats * right[s] + (1.0 - decay_stats) * term

        for n, (value, home) in enumerate(
            ((fresh, out_moment), (new_left, out_left), (new_right, out_right))
        ):
            copy = pltpu.make_async_copy(value.at[s], home.at[s], more.at[n * SLOTS + s])
            copy.start()
            copies.append(copy)
    for copy in copies:
        copy.wait()


def finish_kernel(spot, begun, low_other, high_other, out, sems):
    del begun
    sources = ((6, 0, 2, 1, low_other), (6, 2, 2, 0, high_other))
    copies = placed_copies(spot, sources, out, sems)
    for copy in copies:
        copy.start()
    for copy in copies:
        copy.wait()


def local(
    gradients, block_order, owner_count, stat_left, stat_right, root_left, root_right, momentum
):
    chunk_type = jax.ShapeDtypeStruct((ROWS, BS), half_type)
    pack_type = jax.ShapeDtypeStruct((4, ROWS, BS), half_type)
    stat_type = jax.ShapeDtypeStruct((SLOTS, ROWS, BS), wide_type)
    hold = lax.optimization_barrier

    mine = gradients[0, 0]
    theirs = to_core(mine)
    mine = small_call(half_kernel, jax.ShapeDtypeStruct((HALF, BS), half_type), "half", mine)
    mine, theirs = hold((mine, theirs))
    own, *sends = small_call(
        pair_kernel,
        [jax.ShapeDtypeStruct((ROWS, BS), wide_type)] + [chunk_type] * 3,
        "pair",
        mine,
        theirs,
    )
    sends, order, count, left, right, moment = hold(
        (sends, block_order, owner_count, root_left[0], root_right[0], momentum[0])
    )
    spot, tiles = choices(order, count)
    packs = small_call(pack_kernel, [pack_type] * 4, "packs", spot, left, right, moment)
    got = along(to_x, [own] + sends)

    packs = small_call(
        total_kernel, [pack_type] * 4, "total", *got, *packs, aliases={4: 0, 5: 1, 6: 2, 7: 3}
    )
    row = along(to_u, packs, (2, 1, 3))
    column = along(to_v, small_call(turn_kernel, [pack_type] * 4, "turn", tiles, *row), (2, 1, 3))
    pack = small_call(here_kernel, pack_type, "here", tiles, *column)
    shared, moment = small_call(
        line_kernel,
        [
            jax.ShapeDtypeStruct((X, 3, ROWS, BS), half_type),
            jax.ShapeDtypeStruct((X, ROWS, BS), half_type),
        ],
        "line",
        *along(to_x, [pack] * 4, (2, 1, 3)),
    )
    send = small_call(
        step_kernel,
        jax.ShapeDtypeStruct((6, ROWS, BS), half_type),
        "step",
        shared,
        moment,
        to_core(shared),
        flops=6 * BS**3,
        scratch=[
            pltpu.VMEM((BS, BS), half_type),
            pltpu.VMEM((2, BS, BS), half_type),
            pltpu.VMEM((BS, BS), wide_type),
        ],
    )

    row = along(to_u, [send] * 4, (2, 1, 3))
    near_type = jax.ShapeDtypeStruct((18, ROWS, BS), half_type)
    sent_type = jax.ShapeDtypeStruct((19, ROWS, BS), half_type)
    near, ahead, back = small_call(
        near_kernel, [near_type, sent_type, sent_type], "near", tiles, *row
    )
    one, three = to_v(ahead, 1), to_v(back, 3)
    near_other = to_core(near)
    low = to_v(one[:9], 1)
    high = to_v(three[8:17], 3)
    one_other, three_other = to_core(one), to_core(three)
    begun = place(0, spot, None, near, near_other)
    begun = place(1, spot, begun, one, one_other)
    begun = place(3, spot, begun, three, three_other)
    low, high, begun = hold((low, high, begun))
    low_other, high_other = to_core(low), to_core(high)
    begun, new_momentum, left_stats, right_stats = pl.pallas_call(
        owner_kernel,
        out_shape=[jax.ShapeDtypeStruct(begun.shape, half_type)] + [stat_type] * 3,
        in_specs=[SMEM, ANY] + [VMEM] * 8,
        out_specs=[ANY] * 4,
        scratch_shapes=[pltpu.VMEM((SLOTS, ROWS, BS), wide_type)] * 3
        + [pltpu.SemaphoreType.DMA((4,)), pltpu.SemaphoreType.DMA((3 * SLOTS,))],
        input_output_aliases={1: 0},
        compiler_params=pltpu.CompilerParams(vmem_limit_bytes=8 << 20),
        cost_estimate=cost(0, near, one, three, low, high),
        name="owner",
    )(spot, begun, momentum[0], stat_left[0], stat_right[0], near, one, three, low, high)
    update_blocks = pl.pallas_call(
        finish_kernel,
        out_shape=jax.ShapeDtypeStruct(begun.shape, half_type),
        in_specs=[SMEM, ANY, VMEM, VMEM],
        out_specs=ANY,
        scratch_shapes=[pltpu.SemaphoreType.DMA((4,))],
        input_output_aliases={1: 0},
        compiler_params=pltpu.CompilerParams(vmem_limit_bytes=4 << 20),
        cost_estimate=cost(0, low_other, high_other),
        name="finish",
    )(spot, begun, low_other, high_other)
    update_blocks = update_blocks.reshape(BLOCKS, BS, BS)
    return (update_blocks, left_stats[None], right_stats[None], new_momentum[None])


def solution(mesh):
    placed = (
        P("dp", "group", None, None),
        P(),
        P(),
        P("group", None, "dp", None),
        P("group", None, "dp", None),
        P("group", None, "dp", None),
        P("group", None, "dp", None),
        P("group", None, "dp", None),
    )
    return jax.shard_map(
        local,
        mesh=mesh,
        in_specs=placed,
        out_specs=(
            P(),
            P("group", None, "dp", None),
            P("group", None, "dp", None),
            P("group", None, "dp", None),
        ),
        check_vma=False,
    )
```

```python
import functools

import jax
import jax.numpy as jnp
from jax import lax
from jax.experimental import pallas as pl
from jax.experimental.pallas import tpu as pltpu
from jax.sharding import PartitionSpec as P

decay_stats = 0.95
decay_moment = 0.9
epsilon = 1e-06

AXES = ("dp", "group")
X, CORES, SIDE, SLOTS = 4, 2, 4, 3
BLOCKS = SIDE * SIDE
BS = 512
ROWS = BS // (X * CORES)
HALF = BS // CORES
NEAR = SIDE * HALF
half_type = jnp.bfloat16
wide_type = jnp.float32

SMEM = pl.BlockSpec(memory_space=pltpu.SMEM)
VMEM = pl.BlockSpec(memory_space=pltpu.VMEM)
ANY = pl.BlockSpec(memory_space=pl.ANY)

GRAD_PICK, GRAD_LAST, ROOT_PICK, ROOT_LAST, TERM_PICK, TILES = 0, 4, 5, 9, 10, 14
SLOT_PICK, TERM_LAST, SLOT_LIVE, SLOT_FROM, SLOT_ROW = 14, 18, 21, 24, 27
LANDING = 30
CHOICES = LANDING + 32


def permute(value, target):
    pairs = []
    for x in range(X):
        for c in range(CORES):
            for z in range(SIDE):
                for y in range(SIDE):
                    tx, tc, tz, ty = target(x, c, z, y)
                    pairs.append(
                        ((x * 2 + c) * 16 + z * 4 + y, ((tx % 4) * 2 + tc) * 16 + (tz % 4) * 4 + ty % 4)
                    )
    return lax.ppermute(value, AXES, pairs)


def to_core(value):
    return permute(value, lambda x, c, z, y: (x, 1 - c, z, y))


def to_x(value, k):
    return permute(value, lambda x, c, z, y: (x + k, c, z, y))


def to_u(value, k):
    return permute(value, lambda x, c, z, y: (x, c, z, y + k) if c == 0 else (x, c, z + k, y))


def to_v(value, k):
    return permute(value, lambda x, c, z, y: (x, c, z + k, y) if c == 0 else (x, c, z, y + k))


def along(send, values, shifts=(1, 3, 2)):
    return [values[0]] + [send(values[k], k) for k in shifts]


def position():
    dp, me = lax.axis_index("dp"), lax.axis_index("group")
    return dp >> 1, dp & 1, me >> 2, me & 3


def choice_kernel(order_ref, count_ref, out, tiles, start_ref, owner_ref):
    x, c, z, y = position()
    me = z * 4 + y
    first = c == 0
    u, v = jnp.where(first, y, z), jnp.where(first, z, y)

    def place_at(uu, vv):
        yy, zz = jnp.where(first, uu, vv), jnp.where(first, vv, uu)
        return 4 * ((zz - yy) & 3) + yy

    def uv_of_member(g):
        yy, zz = g & 3, g >> 2
        return jnp.where(first, yy, zz), jnp.where(first, zz, yy)

    def uv_of_place(q):
        yy = q & 3
        zz = (yy + (q >> 2)) & 3
        return jnp.where(first, yy, zz), jnp.where(first, zz, yy)

    place = jnp.int32(0)
    for o in range(BLOCKS):
        start_ref[o] = place
        for s in range(SLOTS):

            @pl.when(s < count_ref[o])
            def _():
                owner_ref[start_ref[o] + s] = o

        place = place + count_ref[o]

    for k in range(4):
        q = place_at(u, (v + k) & 3)
        block = order_ref[q]
        bu, bv = uv_of_member(block)
        out[GRAD_PICK + k] = (u - bu) & 3
        ou, ov = uv_of_member(owner_ref[q])
        out[ROOT_PICK + k] = (u - ou) & 3
        if k == 0:
            out[GRAD_LAST] = (v - bv) & 3
            out[ROOT_LAST] = (v - ov) & 3
    my_start, my_count = start_ref[me], count_ref[me]
    slot_u = []
    for s in range(SLOTS):
        q = jnp.minimum(my_start + s, BLOCKS - 1)
        su, sv = uv_of_place(q)
        slot_u.append(su)
        out[TERM_LAST + s] = (v - sv) & 3
        out[SLOT_LIVE + s] = (s < my_count).astype(jnp.int32)
        out[SLOT_FROM + s] = jnp.where(s < my_count, (v - sv) & 3, 8)
        out[SLOT_ROW + s] = (u - su) & 3
    for k in range(4):
        far = (u + k) & 3
        chosen = jnp.int32(0)
        for s in range(SLOTS):
            chosen = jnp.where((s < my_count) & (slot_u[s] == far), s, chosen)
        out[SLOT_PICK + k] = chosen
        far = (v + k) & 3
        member = jnp.where(first, 4 * far + u, 4 * u + far)
        chosen = jnp.int32(0)
        for s in range(SLOTS):
            fu, fv = uv_of_place(start_ref[member] + s)
            chosen = jnp.where((s < count_ref[member]) & (fv == v), (u - fu) & 3, chosen)
        out[TERM_PICK + k] = chosen
    for k in range(4):
        for j in range(4):
            out[LANDING + k * 4 + j] = order_ref[place_at((u - j) & 3, (v - k) & 3)]
            out[LANDING + 16 + k * 4 + j] = order_ref[place_at((u - k) & 3, (v - j) & 3)]
    for n in range(TILES):
        tiles[n] = jnp.full((16, BS), out[n].astype(wide_type), wide_type).astype(half_type)


def choices(block_order, owner_count):
    return pl.pallas_call(
        choice_kernel,
        out_shape=[
            jax.ShapeDtypeStruct((CHOICES,), jnp.int32),
            jax.ShapeDtypeStruct((TILES, 16, BS), half_type),
        ],
        in_specs=[SMEM, SMEM],
        out_specs=[SMEM, VMEM],
        scratch_shapes=[pltpu.SMEM((BLOCKS,), jnp.int32), pltpu.SMEM((BLOCKS,), jnp.int32)],
        cost_estimate=pl.CostEstimate(flops=0, bytes_accessed=4 << 20, transcendentals=0),
        name="choices",
    )(block_order, owner_count)


def cost(flops, *arrays):
    moved = sum(a.size * a.dtype.itemsize for a in arrays)
    return pl.CostEstimate(flops=flops, bytes_accessed=moved, transcendentals=0)


def small_call(body, outs, name, *args, aliases=None, flops=0, scratch=()):
    return pl.pallas_call(
        body,
        out_shape=outs,
        in_specs=[SMEM if a.dtype == jnp.int32 else VMEM for a in args],
        out_specs=jax.tree.map(lambda _: VMEM, outs),
        scratch_shapes=scratch,
        input_output_aliases=aliases or {},
        compiler_params=pltpu.CompilerParams(vmem_limit_bytes=12 << 20),
        cost_estimate=cost(flops, *args, *jax.tree.leaves(outs)),
        name=name,
    )(*args)


def blend(choice, options):
    rows = options[0].shape[0]
    parts = [option.reshape(rows // 16, 16, BS) for option in options]
    out = parts[3]
    for n in (2, 1, 0):
        out = jnp.where(choice[None] == n, parts[n], out)
    return out.reshape(rows, BS)


def half_kernel(given, out):
    c = position()[1]
    out[...] = given[pl.ds(pl.multiple_of(c * HALF, HALF), HALF), :]


def pair_kernel(mine, theirs, own, *sends):
    x, c, _, _ = position()
    for k in range(4):
        row = ((x + k) & 3) * ROWS
        at = pl.ds(pl.multiple_of(row, ROWS), ROWS)
        far = pl.ds(pl.multiple_of(c * HALF + row, ROWS), ROWS)
        both = mine[at, :].astype(wide_type) + theirs[far, :].astype(wide_type)
        if k == 0:
            own[...] = both
        else:
            sends[k - 1][...] = both.astype(half_type)


def pack_kernel(spot, left, right, moment, *outs):
    for k, out in enumerate(outs):
        slot = spot[SLOT_PICK + k]
        out[0] = left[slot].astype(half_type)
        out[1] = right[slot].astype(half_type)
        out[3] = moment[slot].astype(half_type)


def total_kernel(own, a, c, b, *packs):
    total = own[...] + a[...].astype(wide_type)
    total = total + b[...].astype(wide_type)
    total = (total + c[...].astype(wide_type)).astype(half_type)
    for out in packs[4:]:
        out[2] = total


def turn_kernel(tiles, a, c, b, d, *outs):
    for n in range(4):
        options = [source[n] for source in (a, b, c, d)]
        base = GRAD_PICK if n == 2 else ROOT_PICK
        for k, out in enumerate(outs):
            out[n] = blend(tiles[base + k], options)


def here_kernel(tiles, a, c, b, d, out):
    for n in range(4):
        options = [source[n] for source in (a, b, c, d)]
        out[n] = blend(tiles[GRAD_LAST if n == 2 else ROOT_LAST], options)


def both_kernel(one, three, out):
    out[0] = one[:3]
    out[1] = three[:3]


def step_kernel(own, two, one, three, own_other, two_other, rest_other, out, grad, full, held):
    x, c, _, _ = position()
    others = (own_other, rest_other.at[0], two_other, rest_other.at[1])
    for k, mine in enumerate((own, one, two, three)):
        n = (x - k) & 3
        for core, source in ((c, mine), (1 - c, others[k])):
            rows = pl.ds(pl.multiple_of((2 * n + core) * ROWS, ROWS), ROWS)
            for which in range(2):
                full[which, rows, :] = source[which]
            grad[pl.ds(pl.multiple_of(core * HALF + n * ROWS, ROWS), ROWS), :] = source[2]
    g = grad[...]
    wide = g.astype(wide_type)
    grad_square = jnp.sum(wide * wide)
    precond = jnp.dot(full[0], g, preferred_element_type=wide_type).astype(half_type)
    held[...] = jnp.dot(precond, full[1], preferred_element_type=wide_type)
    dir_square = jnp.sum(held[...] * held[...])
    entries = float(BS * BS)
    top = jnp.sqrt(jnp.full((1, BS), grad_square / entries, wide_type))
    graft = top / jnp.sqrt(jnp.full((1, BS), dir_square / entries + epsilon, wide_type))
    for k, mine in enumerate((own, one, two, three)):
        n = (x - k) & 3
        rows = pl.ds(pl.multiple_of((2 * n + c) * ROWS, ROWS), ROWS)
        fresh = decay_moment * mine[3].astype(wide_type) + graft * held[rows, :]
        out[n] = fresh.astype(half_type)
    rows = grad[pl.ds(pl.multiple_of((2 * x + c) * ROWS, ROWS), ROWS), :]
    out[4] = lax.dot_general(
        rows, g, (((1,), (1,)), ((), ())), preferred_element_type=wide_type
    ).astype(half_type)
    columns = grad[:, pl.ds(pl.multiple_of(x * 2 * ROWS, 2 * ROWS), 2 * ROWS)]
    held[: 2 * ROWS, :] = lax.dot_general(
        columns, g, (((0,), (0,)), ((), ())), preferred_element_type=wide_type
    )
    out[5] = held[pl.ds(pl.multiple_of(c * ROWS, ROWS), ROWS), :].astype(half_type)


def near_kernel(tiles, a, c, b, d, near, ahead, back):
    sources = (a, b, c, d)
    for out, first in ((near, 0), (ahead, 1), (back, 0)):
        for j, source in enumerate(sources):
            out[first + j * 4 : first + j * 4 + 4] = source[:4]
    left = [source[4] for source in sources]
    right = [source[5] for source in sources]
    for k, out, first in ((0, near, 16), (1, ahead, 17), (3, back, 17)):
        out[first] = blend(tiles[TERM_PICK + k], left)
        out[first + 1] = blend(tiles[TERM_PICK + k], right)
    ahead[0] = blend(tiles[TERM_PICK + 2], left)
    back[16] = blend(tiles[TERM_PICK + 2], right)


def placed_copies(spot, sources, out, sems):
    _, c, _, _ = position()
    copies = []
    for which, first, count, skip, source in sources:
        half = c if which < 4 else 1 - c
        for j in range(count):
            copies.append(
                pltpu.make_async_copy(
                    source.at[pl.ds(skip + j * 4, 4)],
                    out.at[spot[LANDING + which * 4 + first + j], :, half],
                    sems.at[len(copies)],
                )
            )
    return copies


def place_kernel(which, spot, *refs):
    mine, other, out, sems = refs[-4:]
    skip = 1 if which == 1 else 0
    sources = ((which, 0, 4, skip, mine), (which + 4, 0, 4, skip, other))
    copies = placed_copies(spot, sources, out, sems)
    for copy in copies:
        copy.start()
    for copy in copies:
        copy.wait()


def place(which, spot, begun, mine, other):
    given = [mine, other] if begun is None else [begun, mine, other]
    return pl.pallas_call(
        functools.partial(place_kernel, which),
        out_shape=jax.ShapeDtypeStruct((BLOCKS, X, CORES, ROWS, BS), half_type),
        in_specs=[SMEM] + [ANY] * (len(given) - 2) + [VMEM] * 2,
        out_specs=ANY,
        scratch_shapes=[pltpu.SemaphoreType.DMA((8,))],
        input_output_aliases={} if begun is None else {1: 0},
        compiler_params=pltpu.CompilerParams(vmem_limit_bytes=4 << 20),
        cost_estimate=cost(0, mine, other, mine, other),
        name="place",
    )(spot, *given)


def owner_kernel(spot, begun, moment, left, right, near, one, three, low, high, *refs):
    del begun
    out, out_moment, out_left, out_right, fresh, new_left, new_right, sems, more = refs
    sources = ((2, 0, 2, 1, low), (2, 2, 2, 0, high))
    copies = placed_copies(spot, sources, out, sems)
    for copy in copies:
        copy.start()
    x = position()[0]
    parts = ((0, 0, 4, 0, near), (1, 0, 4, 1, one), (3, 0, 4, 0, three)) + sources
    terms = ((near, 16, near, 17), (one, 17, one, 18), (low, 0, high, 8), (three, 17, three, 18))
    for s in range(SLOTS):
        fresh[s] = moment[s]
        new_left[s] = left[s]
        new_right[s] = right[s]
        came, place = spot[SLOT_FROM + s], spot[SLOT_ROW + s]
        for which, first, count, skip, source in parts:

            @pl.when((came == which) & (place >= first) & (place < first + count))
            def _():
                fresh[s] = source[skip + (place - first) * 4 + x].astype(wide_type)

        for n, (left_from, m, right_from, r) in enumerate(terms):

            @pl.when((spot[SLOT_LIVE + s] == 1) & (spot[TERM_LAST + s] == n))
            def _():
                term = left_from[m].astype(wide_type)
                new_left[s] = decay_stats * left[s] + (1.0 - decay_stats) * term
                term = right_from[r].astype(wide_type)
                new_right[s] = decay_stats * right[s] + (1.0 - decay_stats) * term

        for n, (value, home) in enumerate(
            ((fresh, out_moment), (new_left, out_left), (new_right, out_right))
        ):
            copy = pltpu.make_async_copy(value.at[s], home.at[s], more.at[n * SLOTS + s])
            copy.start()
            copies.append(copy)
    for copy in copies:
        copy.wait()


def finish_kernel(spot, begun, low_other, high_other, out, sems):
    del begun
    sources = ((6, 0, 2, 0, low_other), (6, 2, 2, 0, high_other))
    copies = placed_copies(spot, sources, out, sems)
    for copy in copies:
        copy.start()
    for copy in copies:
        copy.wait()


def local(
    gradients, block_order, owner_count, stat_left, stat_right, root_left, root_right, momentum
):
    chunk_type = jax.ShapeDtypeStruct((ROWS, BS), half_type)
    pack_type = jax.ShapeDtypeStruct((4, ROWS, BS), half_type)
    stat_type = jax.ShapeDtypeStruct((SLOTS, ROWS, BS), wide_type)
    hold = lax.optimization_barrier

    mine = gradients[0, 0]
    theirs = to_core(mine)
    mine = small_call(half_kernel, jax.ShapeDtypeStruct((HALF, BS), half_type), "half", mine)
    mine, theirs = hold((mine, theirs))
    own, *sends = small_call(
        pair_kernel,
        [jax.ShapeDtypeStruct((ROWS, BS), wide_type)] + [chunk_type] * 3,
        "pair",
        mine,
        theirs,
    )
    sends, order, count, left, right, moment = hold(
        (sends, block_order, owner_count, root_left[0], root_right[0], momentum[0])
    )
    spot, tiles = choices(order, count)
    packs = small_call(pack_kernel, [pack_type] * 4, "packs", spot, left, right, moment)
    got = along(to_x, [own] + sends)

    packs = small_call(
        total_kernel, [pack_type] * 4, "total", *got, *packs, aliases={4: 0, 5: 1, 6: 2, 7: 3}
    )
    row = along(to_u, packs, (2, 1, 3))
    column = along(to_v, small_call(turn_kernel, [pack_type] * 4, "turn", tiles, *row), (2, 1, 3))
    pack = small_call(here_kernel, pack_type, "here", tiles, *column)
    own, two, one, three = along(to_x, [pack] * 4, (2, 1, 3))
    own_other, two_other = to_core(own[:3]), to_core(two[:3])
    one, three, own_other, two_other = hold((one, three, own_other, two_other))
    rest = small_call(
        both_kernel, jax.ShapeDtypeStruct((2, 3, ROWS, BS), half_type), "both", one, three
    )
    send = small_call(
        step_kernel,
        jax.ShapeDtypeStruct((6, ROWS, BS), half_type),
        "step",
        own,
        two,
        one,
        three,
        own_other,
        two_other,
        to_core(rest),
        flops=6 * BS**3,
        scratch=[
            pltpu.VMEM((BS, BS), half_type),
            pltpu.VMEM((2, BS, BS), half_type),
            pltpu.VMEM((BS, BS), wide_type),
        ],
    )

    row = along(to_u, [send] * 4, (2, 1, 3))
    near_type = jax.ShapeDtypeStruct((18, ROWS, BS), half_type)
    sent_type = jax.ShapeDtypeStruct((19, ROWS, BS), half_type)
    near, ahead, back = small_call(
        near_kernel, [near_type, sent_type, sent_type], "near", tiles, *row
    )
    one, three = to_v(ahead, 1), to_v(back, 3)
    near_other = to_core(near)
    low = to_v(one[:9], 1)
    high = to_v(three[8:17], 3)
    begun = place(0, spot, None, near, near_other)
    (far_one, far_three), _ = hold(((one, three), begun))
    one_other, three_other = to_core(far_one), to_core(far_three)
    begun = place(1, spot, begun, one, one_other)
    begun = place(3, spot, begun, three, three_other)
    low, high, begun = hold((low, high, begun))
    low_other, high_other = to_core(low[1:]), to_core(high[:8])
    begun, new_momentum, left_stats, right_stats = pl.pallas_call(
        owner_kernel,
        out_shape=[jax.ShapeDtypeStruct(begun.shape, half_type)] + [stat_type] * 3,
        in_specs=[SMEM, ANY] + [VMEM] * 8,
        out_specs=[ANY] * 4,
        scratch_shapes=[pltpu.VMEM((SLOTS, ROWS, BS), wide_type)] * 3
        + [pltpu.SemaphoreType.DMA((4,)), pltpu.SemaphoreType.DMA((3 * SLOTS,))],
        input_output_aliases={1: 0},
        compiler_params=pltpu.CompilerParams(vmem_limit_bytes=8 << 20),
        cost_estimate=cost(0, near, one, three, low, high),
        name="owner",
    )(spot, begun, momentum[0], stat_left[0], stat_right[0], near, one, three, low, high)
    update_blocks = pl.pallas_call(
        finish_kernel,
        out_shape=jax.ShapeDtypeStruct(begun.shape, half_type),
        in_specs=[SMEM, ANY, VMEM, VMEM],
        out_specs=ANY,
        scratch_shapes=[pltpu.SemaphoreType.DMA((4,))],
        input_output_aliases={1: 0},
        compiler_params=pltpu.CompilerParams(vmem_limit_bytes=4 << 20),
        cost_estimate=cost(0, low_other, high_other),
        name="finish",
    )(spot, begun, low_other, high_other)
    update_blocks = update_blocks.reshape(BLOCKS, BS, BS)
    return (update_blocks, left_stats[None], right_stats[None], new_momentum[None])


def solution(mesh):
    placed = (
        P("dp", "group", None, None),
        P(),
        P(),
        P("group", None, "dp", None),
        P("group", None, "dp", None),
        P("group", None, "dp", None),
        P("group", None, "dp", None),
        P("group", None, "dp", None),
    )
    return jax.shard_map(
        local,
        mesh=mesh,
        in_specs=placed,
        out_specs=(
            P(),
            P("group", None, "dp", None),
            P("group", None, "dp", None),
            P("group", None, "dp", None),
        ),
        check_vma=False,
    )
```

```python
import functools

import jax
import jax.numpy as jnp
from jax import lax
from jax.experimental import pallas as pl
from jax.experimental.pallas import tpu as pltpu
from jax.sharding import PartitionSpec as P

decay_stats = 0.95
decay_moment = 0.9
epsilon = 1e-06

AXES = ("dp", "group")
X, CORES, SIDE, SLOTS = 4, 2, 4, 3
BLOCKS = SIDE * SIDE
BS = 512
ROWS = BS // (X * CORES)
HALF = BS // CORES
NEAR = SIDE * HALF
half_type = jnp.bfloat16
wide_type = jnp.float32

SMEM = pl.BlockSpec(memory_space=pltpu.SMEM)
VMEM = pl.BlockSpec(memory_space=pltpu.VMEM)
ANY = pl.BlockSpec(memory_space=pl.ANY)

GRAD_PICK, GRAD_LAST, ROOT_PICK, ROOT_LAST, TERM_PICK, TILES = 0, 4, 5, 9, 10, 14
SLOT_PICK, TERM_LAST, SLOT_LIVE, SLOT_FROM, SLOT_ROW = 14, 18, 21, 24, 27
LANDING = 30
CHOICES = LANDING + 32


def permute(value, target):
    pairs = []
    for x in range(X):
        for c in range(CORES):
            for z in range(SIDE):
                for y in range(SIDE):
                    tx, tc, tz, ty = target(x, c, z, y)
                    pairs.append(
                        ((x * 2 + c) * 16 + z * 4 + y, ((tx % 4) * 2 + tc) * 16 + (tz % 4) * 4 + ty % 4)
                    )
    return lax.ppermute(value, AXES, pairs)


def to_core(value):
    return permute(value, lambda x, c, z, y: (x, 1 - c, z, y))


def to_x(value, k):
    return permute(value, lambda x, c, z, y: (x + k, c, z, y))


def to_u(value, k):
    return permute(value, lambda x, c, z, y: (x, c, z, y + k) if c == 0 else (x, c, z + k, y))


def to_v(value, k):
    return permute(value, lambda x, c, z, y: (x, c, z + k, y) if c == 0 else (x, c, z, y + k))


def along(send, values, shifts=(1, 3, 2)):
    return [values[0]] + [send(values[k], k) for k in shifts]


def position():
    dp, me = lax.axis_index("dp"), lax.axis_index("group")
    return dp >> 1, dp & 1, me >> 2, me & 3


def choice_kernel(order_ref, count_ref, out, tiles, start_ref, owner_ref):
    x, c, z, y = position()
    me = z * 4 + y
    first = c == 0
    u, v = jnp.where(first, y, z), jnp.where(first, z, y)

    def place_at(uu, vv):
        yy, zz = jnp.where(first, uu, vv), jnp.where(first, vv, uu)
        return 4 * ((zz - yy) & 3) + yy

    def uv_of_member(g):
        yy, zz = g & 3, g >> 2
        return jnp.where(first, yy, zz), jnp.where(first, zz, yy)

    def uv_of_place(q):
        yy = q & 3
        zz = (yy + (q >> 2)) & 3
        return jnp.where(first, yy, zz), jnp.where(first, zz, yy)

    place = jnp.int32(0)
    for o in range(BLOCKS):
        start_ref[o] = place
        for s in range(SLOTS):

            @pl.when(s < count_ref[o])
            def _():
                owner_ref[start_ref[o] + s] = o

        place = place + count_ref[o]

    for k in range(4):
        q = place_at(u, (v + k) & 3)
        block = order_ref[q]
        bu, bv = uv_of_member(block)
        out[GRAD_PICK + k] = (u - bu) & 3
        ou, ov = uv_of_member(owner_ref[q])
        out[ROOT_PICK + k] = (u - ou) & 3
        if k == 0:
            out[GRAD_LAST] = (v - bv) & 3
            out[ROOT_LAST] = (v - ov) & 3
    my_start, my_count = start_ref[me], count_ref[me]
    slot_u = []
    for s in range(SLOTS):
        q = jnp.minimum(my_start + s, BLOCKS - 1)
        su, sv = uv_of_place(q)
        slot_u.append(su)
        out[TERM_LAST + s] = (v - sv) & 3
        out[SLOT_LIVE + s] = (s < my_count).astype(jnp.int32)
        out[SLOT_FROM + s] = jnp.where(s < my_count, (v - sv) & 3, 8)
        out[SLOT_ROW + s] = (u - su) & 3
    for k in range(4):
        far = (u + k) & 3
        chosen = jnp.int32(0)
        for s in range(SLOTS):
            chosen = jnp.where((s < my_count) & (slot_u[s] == far), s, chosen)
        out[SLOT_PICK + k] = chosen
        far = (v + k) & 3
        member = jnp.where(first, 4 * far + u, 4 * u + far)
        chosen = jnp.int32(0)
        for s in range(SLOTS):
            fu, fv = uv_of_place(start_ref[member] + s)
            chosen = jnp.where((s < count_ref[member]) & (fv == v), (u - fu) & 3, chosen)
        out[TERM_PICK + k] = chosen
    for k in range(4):
        for j in range(4):
            out[LANDING + k * 4 + j] = order_ref[place_at((u - j) & 3, (v - k) & 3)]
            out[LANDING + 16 + k * 4 + j] = order_ref[place_at((u - k) & 3, (v - j) & 3)]
    for n in range(TILES):
        tiles[n] = jnp.full((16, BS), out[n].astype(wide_type), wide_type).astype(half_type)


def choices(block_order, owner_count):
    return pl.pallas_call(
        choice_kernel,
        out_shape=[
            jax.ShapeDtypeStruct((CHOICES,), jnp.int32),
            jax.ShapeDtypeStruct((TILES, 16, BS), half_type),
        ],
        in_specs=[SMEM, SMEM],
        out_specs=[SMEM, VMEM],
        scratch_shapes=[pltpu.SMEM((BLOCKS,), jnp.int32), pltpu.SMEM((BLOCKS,), jnp.int32)],
        cost_estimate=pl.CostEstimate(flops=0, bytes_accessed=4 << 20, transcendentals=0),
        name="choices",
    )(block_order, owner_count)


def cost(flops, *arrays):
    moved = sum(a.size * a.dtype.itemsize for a in arrays)
    return pl.CostEstimate(flops=flops, bytes_accessed=moved, transcendentals=0)


def small_call(body, outs, name, *args, aliases=None, flops=0, scratch=()):
    return pl.pallas_call(
        body,
        out_shape=outs,
        in_specs=[SMEM if a.dtype == jnp.int32 else VMEM for a in args],
        out_specs=jax.tree.map(lambda _: VMEM, outs),
        scratch_shapes=scratch,
        input_output_aliases=aliases or {},
        compiler_params=pltpu.CompilerParams(vmem_limit_bytes=12 << 20),
        cost_estimate=cost(flops, *args, *jax.tree.leaves(outs)),
        name=name,
    )(*args)


def blend(choice, options):
    rows = options[0].shape[0]
    parts = [option.reshape(rows // 16, 16, BS) for option in options]
    out = parts[3]
    for n in (2, 1, 0):
        out = jnp.where(choice[None] == n, parts[n], out)
    return out.reshape(rows, BS)


def half_kernel(given, out):
    c = position()[1]
    out[...] = given[pl.ds(pl.multiple_of(c * HALF, HALF), HALF), :]


def pair_kernel(mine, theirs, own, *sends):
    x, c, _, _ = position()
    for k in range(4):
        row = ((x + k) & 3) * ROWS
        at = pl.ds(pl.multiple_of(row, ROWS), ROWS)
        far = pl.ds(pl.multiple_of(c * HALF + row, ROWS), ROWS)
        both = mine[at, :].astype(wide_type) + theirs[far, :].astype(wide_type)
        if k == 0:
            own[...] = both
        else:
            sends[k - 1][...] = both.astype(half_type)


def pack_kernel(spot, left, right, moment, *outs):
    for k, out in enumerate(outs):
        slot = spot[SLOT_PICK + k]
        out[0] = left[slot].astype(half_type)
        out[1] = right[slot].astype(half_type)
        out[3] = moment[slot].astype(half_type)


def total_kernel(own, a, c, b, *packs):
    total = own[...] + a[...].astype(wide_type)
    total = total + b[...].astype(wide_type)
    total = (total + c[...].astype(wide_type)).astype(half_type)
    for out in packs[4:]:
        out[2] = total


def turn_kernel(tiles, a, c, b, d, *outs):
    for n in range(4):
        options = [source[n] for source in (a, b, c, d)]
        base = GRAD_PICK if n == 2 else ROOT_PICK
        for k, out in enumerate(outs):
            out[n] = blend(tiles[base + k], options)


def here_kernel(tiles, a, c, b, d, out):
    for n in range(4):
        options = [source[n] for source in (a, b, c, d)]
        out[n] = blend(tiles[GRAD_LAST if n == 2 else ROOT_LAST], options)


def both_kernel(one, three, out):
    out[0] = one[:3]
    out[1] = three[:3]


def step_kernel(own, two, one, three, own_other, two_other, rest_other, out, grad, full, held):
    x, c, _, _ = position()
    others = (own_other, rest_other.at[0], two_other, rest_other.at[1])
    for k, mine in enumerate((own, one, two, three)):
        n = (x - k) & 3
        for core, source in ((c, mine), (1 - c, others[k])):
            rows = pl.ds(pl.multiple_of((2 * n + core) * ROWS, ROWS), ROWS)
            for which in range(2):
                full[which, rows, :] = source[which]
            grad[pl.ds(pl.multiple_of(core * HALF + n * ROWS, ROWS), ROWS), :] = source[2]
    g = grad[...]
    wide = g.astype(wide_type)
    grad_square = jnp.sum(wide * wide)
    precond = jnp.dot(full[0], g, preferred_element_type=wide_type).astype(half_type)
    direction = jnp.dot(precond, full[1], preferred_element_type=wide_type)
    dir_square = jnp.sum(direction * direction)
    held[...] = direction
    entries = float(BS * BS)
    top = jnp.sqrt(jnp.full((1, BS), grad_square / entries, wide_type))
    graft = top / jnp.sqrt(jnp.full((1, BS), dir_square / entries + epsilon, wide_type))
    for k, mine in enumerate((own, one, two, three)):
        n = (x - k) & 3
        rows = pl.ds(pl.multiple_of((2 * n + c) * ROWS, ROWS), ROWS)
        fresh = decay_moment * mine[3].astype(wide_type) + graft * held[rows, :]
        out[n] = fresh.astype(half_type)
    rows = grad[pl.ds(pl.multiple_of((2 * x + c) * ROWS, ROWS), ROWS), :]
    out[4] = lax.dot_general(
        rows, g, (((1,), (1,)), ((), ())), preferred_element_type=wide_type
    ).astype(half_type)
    columns = grad[:, pl.ds(pl.multiple_of(x * 2 * ROWS, 2 * ROWS), 2 * ROWS)]
    held[: 2 * ROWS, :] = lax.dot_general(
        columns, g, (((0,), (0,)), ((), ())), preferred_element_type=wide_type
    )
    out[5] = held[pl.ds(pl.multiple_of(c * ROWS, ROWS), ROWS), :].astype(half_type)


def near_kernel(tiles, a, c, b, d, terms, ahead, back):
    sources = (a, b, c, d)
    for out, first in ((ahead, 1), (back, 0)):
        for j, source in enumerate(sources):
            out[first + j * 4 : first + j * 4 + 4] = source[:4]
    left = [source[4] for source in sources]
    right = [source[5] for source in sources]
    for k, out, first in ((0, terms, 0), (1, ahead, 17), (3, back, 17)):
        out[first] = blend(tiles[TERM_PICK + k], left)
        out[first + 1] = blend(tiles[TERM_PICK + k], right)
    ahead[0] = blend(tiles[TERM_PICK + 2], left)
    back[16] = blend(tiles[TERM_PICK + 2], right)


def placed_copies(spot, sources, out, sems):
    _, c, _, _ = position()
    copies = []
    for which, first, count, skip, source in sources:
        half = c if which < 4 else 1 - c
        for j in range(count):
            copies.append(
                pltpu.make_async_copy(
                    source.at[pl.ds(skip + j * 4, 4)],
                    out.at[spot[LANDING + which * 4 + first + j], :, half],
                    sems.at[len(copies)],
                )
            )
    return copies


def place_kernel(which, spot, *refs):
    mine, other, out, sems = refs[-4:]
    skip = 1 if which < 3 else 0
    sources = ((which, 0, 4, skip, mine), (which + 4, 0, 4, skip, other))
    copies = placed_copies(spot, sources, out, sems)
    for copy in copies:
        copy.start()
    for copy in copies:
        copy.wait()


def place(which, spot, begun, mine, other):
    given = [mine, other] if begun is None else [begun, mine, other]
    return pl.pallas_call(
        functools.partial(place_kernel, which),
        out_shape=jax.ShapeDtypeStruct((BLOCKS, X, CORES, ROWS, BS), half_type),
        in_specs=[SMEM] + [ANY] * (len(given) - 2) + [VMEM] * 2,
        out_specs=ANY,
        scratch_shapes=[pltpu.SemaphoreType.DMA((8,))],
        input_output_aliases={} if begun is None else {1: 0},
        compiler_params=pltpu.CompilerParams(vmem_limit_bytes=4 << 20),
        cost_estimate=cost(0, mine, other, mine, other),
        name="place",
    )(spot, *given)


def owner_kernel(spot, begun, moment, left, right, near, own, one, three, low, high, *refs):
    del begun
    out, out_moment, out_left, out_right, fresh, new_left, new_right, sems, more = refs
    sources = ((2, 0, 2, 1, low), (2, 2, 2, 0, high))
    copies = placed_copies(spot, sources, out, sems)
    for copy in copies:
        copy.start()
    x = position()[0]
    parts = ((0, 0, 4, 1, near), (1, 0, 4, 1, one), (3, 0, 4, 0, three)) + sources
    terms = ((own, 0, own, 1), (one, 17, one, 18), (low, 0, high, 8), (three, 17, three, 18))
    for s in range(SLOTS):
        fresh[s] = moment[s]
        new_left[s] = left[s]
        new_right[s] = right[s]
        came, place = spot[SLOT_FROM + s], spot[SLOT_ROW + s]
        for which, first, count, skip, source in parts:

            @pl.when((came == which) & (place >= first) & (place < first + count))
            def _():
                fresh[s] = source[skip + (place - first) * 4 + x].astype(wide_type)

        for n, (left_from, m, right_from, r) in enumerate(terms):

            @pl.when((spot[SLOT_LIVE + s] == 1) & (spot[TERM_LAST + s] == n))
            def _():
                term = left_from[m].astype(wide_type)
                new_left[s] = decay_stats * left[s] + (1.0 - decay_stats) * term
                term = right_from[r].astype(wide_type)
                new_right[s] = decay_stats * right[s] + (1.0 - decay_stats) * term

        for n, (value, home) in enumerate(
            ((fresh, out_moment), (new_left, out_left), (new_right, out_right))
        ):
            copy = pltpu.make_async_copy(value.at[s], home.at[s], more.at[n * SLOTS + s])
            copy.start()
            copies.append(copy)
    for copy in copies:
        copy.wait()


def finish_kernel(spot, begun, low_other, high_other, out, sems):
    del begun
    sources = ((6, 0, 2, 0, low_other), (6, 2, 2, 0, high_other))
    copies = placed_copies(spot, sources, out, sems)
    for copy in copies:
        copy.start()
    for copy in copies:
        copy.wait()


def local(
    gradients, block_order, owner_count, stat_left, stat_right, root_left, root_right, momentum
):
    chunk_type = jax.ShapeDtypeStruct((ROWS, BS), half_type)
    pack_type = jax.ShapeDtypeStruct((4, ROWS, BS), half_type)
    stat_type = jax.ShapeDtypeStruct((SLOTS, ROWS, BS), wide_type)
    hold = lax.optimization_barrier

    mine = gradients[0, 0]
    theirs = to_core(mine)
    mine = small_call(half_kernel, jax.ShapeDtypeStruct((HALF, BS), half_type), "half", mine)
    mine, theirs = hold((mine, theirs))
    own, *sends = small_call(
        pair_kernel,
        [jax.ShapeDtypeStruct((ROWS, BS), wide_type)] + [chunk_type] * 3,
        "pair",
        mine,
        theirs,
    )
    sends, order, count, left, right, moment = hold(
        (sends, block_order, owner_count, root_left[0], root_right[0], momentum[0])
    )
    spot, tiles = choices(order, count)
    packs = small_call(pack_kernel, [pack_type] * 4, "packs", spot, left, right, moment)
    got = along(to_x, [own] + sends)

    packs = small_call(
        total_kernel, [pack_type] * 4, "total", *got, *packs, aliases={4: 0, 5: 1, 6: 2, 7: 3}
    )
    row = along(to_u, packs, (2, 1, 3))
    column = along(to_v, small_call(turn_kernel, [pack_type] * 4, "turn", tiles, *row), (2, 1, 3))
    pack = small_call(here_kernel, pack_type, "here", tiles, *column)
    own, two, one, three = along(to_x, [pack] * 4, (2, 1, 3))
    own_other, two_other = to_core(own[:3]), to_core(two[:3])
    one, three, own_other, two_other = hold((one, three, own_other, two_other))
    rest = small_call(
        both_kernel, jax.ShapeDtypeStruct((2, 3, ROWS, BS), half_type), "both", one, three
    )
    send = small_call(
        step_kernel,
        jax.ShapeDtypeStruct((6, ROWS, BS), half_type),
        "step",
        own,
        two,
        one,
        three,
        own_other,
        two_other,
        to_core(rest),
        flops=6 * BS**3,
        scratch=[
            pltpu.VMEM((BS, BS), half_type),
            pltpu.VMEM((2, BS, BS), half_type),
            pltpu.VMEM((BS, BS), wide_type),
        ],
    )

    row = along(to_u, [send] * 4, (2, 1, 3))
    terms_type = jax.ShapeDtypeStruct((2, ROWS, BS), half_type)
    sent_type = jax.ShapeDtypeStruct((19, ROWS, BS), half_type)
    terms, near, back = small_call(
        near_kernel, [terms_type, sent_type, sent_type], "near", tiles, *row
    )
    one, three = to_v(near, 1), to_v(back, 3)
    near_other = to_core(near)
    low = to_v(one[:9], 1)
    high = to_v(three[8:17], 3)
    begun = place(0, spot, None, near, near_other)
    (far_one, far_three), _ = hold(((one, three), begun))
    one_other, three_other = to_core(far_one), to_core(far_three)
    begun = place(1, spot, begun, one, one_other)
    begun = place(3, spot, begun, three, three_other)
    low, high, begun = hold((low, high, begun))
    low_other, high_other = to_core(low[1:]), to_core(high[:8])
    begun, new_momentum, left_stats, right_stats = pl.pallas_call(
        owner_kernel,
        out_shape=[jax.ShapeDtypeStruct(begun.shape, half_type)] + [stat_type] * 3,
        in_specs=[SMEM, ANY] + [VMEM] * 9,
        out_specs=[ANY] * 4,
        scratch_shapes=[pltpu.VMEM((SLOTS, ROWS, BS), wide_type)] * 3
        + [pltpu.SemaphoreType.DMA((4,)), pltpu.SemaphoreType.DMA((3 * SLOTS,))],
        input_output_aliases={1: 0},
        compiler_params=pltpu.CompilerParams(vmem_limit_bytes=8 << 20),
        cost_estimate=cost(0, near, one, three, low, high),
        name="owner",
    )(spot, begun, momentum[0], stat_left[0], stat_right[0], near, terms, one, three, low, high)
    update_blocks = pl.pallas_call(
        finish_kernel,
        out_shape=jax.ShapeDtypeStruct(begun.shape, half_type),
        in_specs=[SMEM, ANY, VMEM, VMEM],
        out_specs=ANY,
        scratch_shapes=[pltpu.SemaphoreType.DMA((4,))],
        input_output_aliases={1: 0},
        compiler_params=pltpu.CompilerParams(vmem_limit_bytes=4 << 20),
        cost_estimate=cost(0, low_other, high_other),
        name="finish",
    )(spot, begun, low_other, high_other)
    update_blocks = update_blocks.reshape(BLOCKS, BS, BS)
    return (update_blocks, left_stats[None], right_stats[None], new_momentum[None])


def solution(mesh):
    placed = (
        P("dp", "group", None, None),
        P(),
        P(),
        P("group", None, "dp", None),
        P("group", None, "dp", None),
        P("group", None, "dp", None),
        P("group", None, "dp", None),
        P("group", None, "dp", None),
    )
    return jax.shard_map(
        local,
        mesh=mesh,
        in_specs=placed,
        out_specs=(
            P(),
            P("group", None, "dp", None),
            P("group", None, "dp", None),
            P("group", None, "dp", None),
        ),
        check_vma=False,
    )
```

```python
import functools

import jax
import jax.numpy as jnp
from jax import lax
from jax.experimental import pallas as pl
from jax.experimental.pallas import tpu as pltpu
from jax.sharding import PartitionSpec as P

decay_stats = 0.95
decay_moment = 0.9
epsilon = 1e-06

AXES = ("dp", "group")
X, CORES, SIDE, SLOTS = 4, 2, 4, 3
BLOCKS = SIDE * SIDE
BS = 512
ROWS = BS // (X * CORES)
HALF = BS // CORES
NEAR = SIDE * HALF
half_type = jnp.bfloat16
wide_type = jnp.float32

SMEM = pl.BlockSpec(memory_space=pltpu.SMEM)
VMEM = pl.BlockSpec(memory_space=pltpu.VMEM)
ANY = pl.BlockSpec(memory_space=pl.ANY)

GRAD_PICK, GRAD_LAST, ROOT_PICK, ROOT_LAST, TERM_PICK, TILES = 0, 4, 5, 9, 10, 14
SLOT_PICK, TERM_LAST, SLOT_LIVE, SLOT_FROM, SLOT_ROW = 14, 18, 21, 24, 27
LANDING = 30
CHOICES = LANDING + 32


def permute(value, target):
    pairs = []
    for x in range(X):
        for c in range(CORES):
            for z in range(SIDE):
                for y in range(SIDE):
                    tx, tc, tz, ty = target(x, c, z, y)
                    pairs.append(
                        ((x * 2 + c) * 16 + z * 4 + y, ((tx % 4) * 2 + tc) * 16 + (tz % 4) * 4 + ty % 4)
                    )
    return lax.ppermute(value, AXES, pairs)


def to_core(value):
    return permute(value, lambda x, c, z, y: (x, 1 - c, z, y))


def to_x(value, k):
    return permute(value, lambda x, c, z, y: (x + k, c, z, y))


def to_u(value, k):
    return permute(value, lambda x, c, z, y: (x, c, z, y + k) if c == 1 else (x, c, z + k, y))


def to_v(value, k):
    return permute(value, lambda x, c, z, y: (x, c, z + k, y) if c == 1 else (x, c, z, y + k))


def along(send, values, shifts=(1, 3, 2)):
    return [values[0]] + [send(values[k], k) for k in shifts]


def position():
    dp, me = lax.axis_index("dp"), lax.axis_index("group")
    return dp >> 1, dp & 1, me >> 2, me & 3


def choice_kernel(order_ref, count_ref, out, tiles, start_ref, owner_ref):
    x, c, z, y = position()
    me = z * 4 + y
    first = c == 1
    u, v = jnp.where(first, y, z), jnp.where(first, z, y)

    def place_at(uu, vv):
        yy, zz = jnp.where(first, uu, vv), jnp.where(first, vv, uu)
        return 4 * ((zz - yy) & 3) + yy

    def uv_of_member(g):
        yy, zz = g & 3, g >> 2
        return jnp.where(first, yy, zz), jnp.where(first, zz, yy)

    def uv_of_place(q):
        yy = q & 3
        zz = (yy + (q >> 2)) & 3
        return jnp.where(first, yy, zz), jnp.where(first, zz, yy)

    place = jnp.int32(0)
    for o in range(BLOCKS):
        start_ref[o] = place
        for s in range(SLOTS):

            @pl.when(s < count_ref[o])
            def _():
                owner_ref[start_ref[o] + s] = o

        place = place + count_ref[o]

    for k in range(4):
        q = place_at(u, (v + k) & 3)
        block = order_ref[q]
        bu, bv = uv_of_member(block)
        out[GRAD_PICK + k] = (u - bu) & 3
        ou, ov = uv_of_member(owner_ref[q])
        out[ROOT_PICK + k] = (u - ou) & 3
        if k == 0:
            out[GRAD_LAST] = (v - bv) & 3
            out[ROOT_LAST] = (v - ov) & 3
    my_start, my_count = start_ref[me], count_ref[me]
    slot_u = []
    for s in range(SLOTS):
        q = jnp.minimum(my_start + s, BLOCKS - 1)
        su, sv = uv_of_place(q)
        slot_u.append(su)
        out[TERM_LAST + s] = (v - sv) & 3
        out[SLOT_LIVE + s] = (s < my_count).astype(jnp.int32)
        out[SLOT_FROM + s] = jnp.where(s < my_count, (v - sv) & 3, 8)
        out[SLOT_ROW + s] = (u - su) & 3
    for k in range(4):
        far = (u + k) & 3
        chosen = jnp.int32(0)
        for s in range(SLOTS):
            chosen = jnp.where((s < my_count) & (slot_u[s] == far), s, chosen)
        out[SLOT_PICK + k] = chosen
        far = (v + k) & 3
        member = jnp.where(first, 4 * far + u, 4 * u + far)
        chosen = jnp.int32(0)
        for s in range(SLOTS):
            fu, fv = uv_of_place(start_ref[member] + s)
            chosen = jnp.where((s < count_ref[member]) & (fv == v), (u - fu) & 3, chosen)
        out[TERM_PICK + k] = chosen
    for k in range(4):
        for j in range(4):
            out[LANDING + k * 4 + j] = order_ref[place_at((u - j) & 3, (v - k) & 3)]
            out[LANDING + 16 + k * 4 + j] = order_ref[place_at((u - k) & 3, (v - j) & 3)]
    for n in range(TILES):
        tiles[n] = jnp.full((16, BS), out[n].astype(wide_type), wide_type).astype(half_type)


def choices(block_order, owner_count):
    return pl.pallas_call(
        choice_kernel,
        out_shape=[
            jax.ShapeDtypeStruct((CHOICES,), jnp.int32),
            jax.ShapeDtypeStruct((TILES, 16, BS), half_type),
        ],
        in_specs=[SMEM, SMEM],
        out_specs=[SMEM, VMEM],
        scratch_shapes=[pltpu.SMEM((BLOCKS,), jnp.int32), pltpu.SMEM((BLOCKS,), jnp.int32)],
        cost_estimate=pl.CostEstimate(flops=0, bytes_accessed=4 << 20, transcendentals=0),
        name="choices",
    )(block_order, owner_count)


def cost(flops, *arrays):
    moved = sum(a.size * a.dtype.itemsize for a in arrays)
    return pl.CostEstimate(flops=flops, bytes_accessed=moved, transcendentals=0)


def small_call(body, outs, name, *args, aliases=None, flops=0, scratch=()):
    return pl.pallas_call(
        body,
        out_shape=outs,
        in_specs=[SMEM if a.dtype == jnp.int32 else VMEM for a in args],
        out_specs=jax.tree.map(lambda _: VMEM, outs),
        scratch_shapes=scratch,
        input_output_aliases=aliases or {},
        compiler_params=pltpu.CompilerParams(vmem_limit_bytes=12 << 20),
        cost_estimate=cost(flops, *args, *jax.tree.leaves(outs)),
        name=name,
    )(*args)


def blend(choice, options):
    rows = options[0].shape[0]
    parts = [option.reshape(rows // 16, 16, BS) for option in options]
    out = parts[3]
    for n in (2, 1, 0):
        out = jnp.where(choice[None] == n, parts[n], out)
    return out.reshape(rows, BS)


def half_kernel(given, out):
    c = position()[1]
    out[...] = given[pl.ds(pl.multiple_of(c * HALF, HALF), HALF), :]


def pair_kernel(mine, theirs, own, *sends):
    x, c, _, _ = position()
    for k in range(4):
        row = ((x + k) & 3) * ROWS
        at = pl.ds(pl.multiple_of(row, ROWS), ROWS)
        far = pl.ds(pl.multiple_of(c * HALF + row, ROWS), ROWS)
        both = mine[at, :].astype(wide_type) + theirs[far, :].astype(wide_type)
        if k == 0:
            own[...] = both
        else:
            sends[k - 1][...] = both.astype(half_type)


def pack_kernel(spot, left, right, moment, *outs):
    for k, out in enumerate(outs):
        slot = spot[SLOT_PICK + k]
        out[0] = left[slot].astype(half_type)
        out[1] = right[slot].astype(half_type)
        out[3] = moment[slot].astype(half_type)


def total_kernel(own, a, c, b, *packs):
    total = own[...] + a[...].astype(wide_type)
    total = total + b[...].astype(wide_type)
    total = (total + c[...].astype(wide_type)).astype(half_type)
    for out in packs[4:]:
        out[2] = total


def turn_kernel(tiles, a, c, b, d, *outs):
    for n in range(4):
        options = [source[n] for source in (a, b, c, d)]
        base = GRAD_PICK if n == 2 else ROOT_PICK
        for k, out in enumerate(outs):
            out[n] = blend(tiles[base + k], options)


def here_kernel(tiles, a, c, b, d, out):
    for n in range(4):
        options = [source[n] for source in (a, b, c, d)]
        out[n] = blend(tiles[GRAD_LAST if n == 2 else ROOT_LAST], options)


def both_kernel(one, three, out):
    out[0] = one[:3]
    out[1] = three[:3]


def step_kernel(own, two, one, three, own_other, two_other, rest_other, out, grad, full, held):
    x, c, _, _ = position()
    others = (own_other, rest_other.at[0], two_other, rest_other.at[1])
    for k, mine in enumerate((own, one, two, three)):
        n = (x - k) & 3
        for core, source in ((c, mine), (1 - c, others[k])):
            rows = pl.ds(pl.multiple_of((2 * n + core) * ROWS, ROWS), ROWS)
            for which in range(2):
                full[which, rows, :] = source[which]
            grad[pl.ds(pl.multiple_of(core * HALF + n * ROWS, ROWS), ROWS), :] = source[2]
    g = grad[...]
    wide = g.astype(wide_type)
    grad_square = jnp.sum(wide * wide)
    precond = jnp.dot(full[0], g, preferred_element_type=wide_type).astype(half_type)
    held[...] = jnp.dot(precond, full[1], preferred_element_type=wide_type)
    dir_square = jnp.sum(held[...] * held[...])
    entries = float(BS * BS)
    top = jnp.sqrt(jnp.full((1, BS), grad_square / entries, wide_type))
    graft = top / jnp.sqrt(jnp.full((1, BS), dir_square / entries + epsilon, wide_type))
    for k, mine in enumerate((own, one, two, three)):
        n = (x - k) & 3
        rows = pl.ds(pl.multiple_of((2 * n + c) * ROWS, ROWS), ROWS)
        fresh = decay_moment * mine[3].astype(wide_type) + graft * held[rows, :]
        out[n] = fresh.astype(half_type)
    rows = grad[pl.ds(pl.multiple_of((2 * x + c) * ROWS, ROWS), ROWS), :]
    out[4] = lax.dot_general(
        rows, g, (((1,), (1,)), ((), ())), preferred_element_type=wide_type
    ).astype(half_type)
    columns = grad[:, pl.ds(pl.multiple_of(x * 2 * ROWS, 2 * ROWS), 2 * ROWS)]
    held[: 2 * ROWS, :] = lax.dot_general(
        columns, g, (((0,), (0,)), ((), ())), preferred_element_type=wide_type
    )
    out[5] = held[pl.ds(pl.multiple_of(c * ROWS, ROWS), ROWS), :].astype(half_type)


def near_kernel(tiles, a, c, b, d, near, ahead, back):
    sources = (a, b, c, d)
    for out, first in ((near, 0), (ahead, 1), (back, 0)):
        for j, source in enumerate(sources):
            out[first + j * 4 : first + j * 4 + 4] = source[:4]
    left = [source[4] for source in sources]
    right = [source[5] for source in sources]
    for k, out, first in ((0, near, 16), (1, ahead, 17), (3, back, 17)):
        out[first] = blend(tiles[TERM_PICK + k], left)
        out[first + 1] = blend(tiles[TERM_PICK + k], right)
    ahead[0] = blend(tiles[TERM_PICK + 2], left)
    back[16] = blend(tiles[TERM_PICK + 2], right)


def placed_copies(spot, sources, out, sems):
    _, c, _, _ = position()
    copies = []
    for which, first, count, skip, source in sources:
        half = c if which < 4 else 1 - c
        for j in range(count):
            copies.append(
                pltpu.make_async_copy(
                    source.at[pl.ds(skip + j * 4, 4)],
                    out.at[spot[LANDING + which * 4 + first + j], :, half],
                    sems.at[len(copies)],
                )
            )
    return copies


def place_kernel(which, spot, *refs):
    mine, other, out, sems = refs[-4:]
    skip = 1 if which == 1 else 0
    sources = ((which, 0, 4, skip, mine), (which + 4, 0, 4, skip, other))
    copies = placed_copies(spot, sources, out, sems)
    for copy in copies:
        copy.start()
    for copy in copies:
        copy.wait()


def place(which, spot, begun, mine, other):
    given = [mine, other] if begun is None else [begun, mine, other]
    return pl.pallas_call(
        functools.partial(place_kernel, which),
        out_shape=jax.ShapeDtypeStruct((BLOCKS, X, CORES, ROWS, BS), half_type),
        in_specs=[SMEM] + [ANY] * (len(given) - 2) + [VMEM] * 2,
        out_specs=ANY,
        scratch_shapes=[pltpu.SemaphoreType.DMA((8,))],
        input_output_aliases={} if begun is None else {1: 0},
        compiler_params=pltpu.CompilerParams(vmem_limit_bytes=4 << 20),
        cost_estimate=cost(0, mine, other, mine, other),
        name="place",
    )(spot, *given)


def owner_kernel(spot, begun, moment, left, right, near, one, three, low, high, *refs):
    del begun
    out, out_moment, out_left, out_right, fresh, new_left, new_right, sems, more = refs
    sources = ((2, 0, 2, 1, low), (2, 2, 2, 0, high))
    copies = placed_copies(spot, sources, out, sems)
    for copy in copies:
        copy.start()
    x = position()[0]
    parts = ((0, 0, 4, 0, near), (1, 0, 4, 1, one), (3, 0, 4, 0, three)) + sources
    terms = ((near, 16, near, 17), (one, 17, one, 18), (low, 0, high, 8), (three, 17, three, 18))
    for s in range(SLOTS):
        fresh[s] = moment[s]
        new_left[s] = left[s]
        new_right[s] = right[s]
        came, place = spot[SLOT_FROM + s], spot[SLOT_ROW + s]
        for which, first, count, skip, source in parts:

            @pl.when((came == which) & (place >= first) & (place < first + count))
            def _():
                fresh[s] = source[skip + (place - first) * 4 + x].astype(wide_type)

        for n, (left_from, m, right_from, r) in enumerate(terms):

            @pl.when((spot[SLOT_LIVE + s] == 1) & (spot[TERM_LAST + s] == n))
            def _():
                term = left_from[m].astype(wide_type)
                new_left[s] = decay_stats * left[s] + (1.0 - decay_stats) * term
                term = right_from[r].astype(wide_type)
                new_right[s] = decay_stats * right[s] + (1.0 - decay_stats) * term

        for n, (value, home) in enumerate(
            ((fresh, out_moment), (new_left, out_left), (new_right, out_right))
        ):
            copy = pltpu.make_async_copy(value.at[s], home.at[s], more.at[n * SLOTS + s])
            copy.start()
            copies.append(copy)
    for copy in copies:
        copy.wait()


def finish_kernel(spot, begun, low_other, high_other, out, sems):
    del begun
    sources = ((6, 0, 2, 0, low_other), (6, 2, 2, 0, high_other))
    copies = placed_copies(spot, sources, out, sems)
    for copy in copies:
        copy.start()
    for copy in copies:
        copy.wait()


def local(
    gradients, block_order, owner_count, stat_left, stat_right, root_left, root_right, momentum
):
    chunk_type = jax.ShapeDtypeStruct((ROWS, BS), half_type)
    pack_type = jax.ShapeDtypeStruct((4, ROWS, BS), half_type)
    stat_type = jax.ShapeDtypeStruct((SLOTS, ROWS, BS), wide_type)
    hold = lax.optimization_barrier

    mine = gradients[0, 0]
    theirs = to_core(mine)
    mine = small_call(half_kernel, jax.ShapeDtypeStruct((HALF, BS), half_type), "half", mine)
    mine, theirs = hold((mine, theirs))
    own, *sends = small_call(
        pair_kernel,
        [jax.ShapeDtypeStruct((ROWS, BS), wide_type)] + [chunk_type] * 3,
        "pair",
        mine,
        theirs,
    )
    sends, order, count, left, right, moment = hold(
        (sends, block_order, owner_count, root_left[0], root_right[0], momentum[0])
    )
    spot, tiles = choices(order, count)
    packs = small_call(pack_kernel, [pack_type] * 4, "packs", spot, left, right, moment)
    got = along(to_x, [own] + sends)

    packs = small_call(
        total_kernel, [pack_type] * 4, "total", *got, *packs, aliases={4: 0, 5: 1, 6: 2, 7: 3}
    )
    row = along(to_u, packs, (2, 1, 3))
    column = along(to_v, small_call(turn_kernel, [pack_type] * 4, "turn", tiles, *row), (2, 1, 3))
    pack = small_call(here_kernel, pack_type, "here", tiles, *column)
    own, two, one, three = along(to_x, [pack] * 4, (2, 1, 3))
    own_other, two_other = to_core(own[:3]), to_core(two[:3])
    one, three, own_other, two_other = hold((one, three, own_other, two_other))
    rest = small_call(
        both_kernel, jax.ShapeDtypeStruct((2, 3, ROWS, BS), half_type), "both", one, three
    )
    send = small_call(
        step_kernel,
        jax.ShapeDtypeStruct((6, ROWS, BS), half_type),
        "step",
        own,
        two,
        one,
        three,
        own_other,
        two_other,
        to_core(rest),
        flops=6 * BS**3,
        scratch=[
            pltpu.VMEM((BS, BS), half_type),
            pltpu.VMEM((2, BS, BS), half_type),
            pltpu.VMEM((BS, BS), wide_type),
        ],
    )

    row = along(to_u, [send] * 4, (2, 1, 3))
    near_type = jax.ShapeDtypeStruct((18, ROWS, BS), half_type)
    sent_type = jax.ShapeDtypeStruct((19, ROWS, BS), half_type)
    near, ahead, back = small_call(
        near_kernel, [near_type, sent_type, sent_type], "near", tiles, *row
    )
    one, three = to_v(ahead, 1), to_v(back, 3)
    near_other = to_core(near)
    low = to_v(one[:9], 1)
    high = to_v(three[8:17], 3)
    begun = place(0, spot, None, near, near_other)
    (far_one, far_three), _ = hold(((one, three), begun))
    one_other, three_other = to_core(far_one), to_core(far_three)
    begun = place(1, spot, begun, one, one_other)
    begun = place(3, spot, begun, three, three_other)
    low, high, begun = hold((low, high, begun))
    low_other, high_other = to_core(low[1:]), to_core(high[:8])
    begun, new_momentum, left_stats, right_stats = pl.pallas_call(
        owner_kernel,
        out_shape=[jax.ShapeDtypeStruct(begun.shape, half_type)] + [stat_type] * 3,
        in_specs=[SMEM, ANY] + [VMEM] * 8,
        out_specs=[ANY] * 4,
        scratch_shapes=[pltpu.VMEM((SLOTS, ROWS, BS), wide_type)] * 3
        + [pltpu.SemaphoreType.DMA((4,)), pltpu.SemaphoreType.DMA((3 * SLOTS,))],
        input_output_aliases={1: 0},
        compiler_params=pltpu.CompilerParams(vmem_limit_bytes=8 << 20),
        cost_estimate=cost(0, near, one, three, low, high),
        name="owner",
    )(spot, begun, momentum[0], stat_left[0], stat_right[0], near, one, three, low, high)
    update_blocks = pl.pallas_call(
        finish_kernel,
        out_shape=jax.ShapeDtypeStruct(begun.shape, half_type),
        in_specs=[SMEM, ANY, VMEM, VMEM],
        out_specs=ANY,
        scratch_shapes=[pltpu.SemaphoreType.DMA((4,))],
        input_output_aliases={1: 0},
        compiler_params=pltpu.CompilerParams(vmem_limit_bytes=4 << 20),
        cost_estimate=cost(0, low_other, high_other),
        name="finish",
    )(spot, begun, low_other, high_other)
    update_blocks = update_blocks.reshape(BLOCKS, BS, BS)
    return (update_blocks, left_stats[None], right_stats[None], new_momentum[None])


def solution(mesh):
    placed = (
        P("dp", "group", None, None),
        P(),
        P(),
        P("group", None, "dp", None),
        P("group", None, "dp", None),
        P("group", None, "dp", None),
        P("group", None, "dp", None),
        P("group", None, "dp", None),
    )
    return jax.shard_map(
        local,
        mesh=mesh,
        in_specs=placed,
        out_specs=(
            P(),
            P("group", None, "dp", None),
            P("group", None, "dp", None),
            P("group", None, "dp", None),
        ),
        check_vma=False,
    )
```
